256 devices in a mesh: ax: 2 (over core), rad: 16 (over y, x), span: 8 (over z).
Axes of the slice: x: 4, y: 4, z: 8, core: 2. Of those that a mesh axis runs over, the one named last changes fastest.
Arguments:
- tensor: float32 [1024, 64, 32, 128], P('ax', 'rad', 'span'), may hold values from -6 to 6
- radial_factor: float32 [64, 16], P('rad'), may hold values from -1 to 1
- span_factor: float32 [32, 16], P('span'), may hold values from -1.5 to 1.5
- start_factor: float32 [1024, 128], P('ax'), may hold values from -0.1875 to 0.1875
Outputs:
- core_block: float32 [128, 16, 16, 128], P(None, 'rad', 'span')
The draws below stay inside these ranges and needn't reach their ends.
All inputs are finite; a program needn't handle non-finite values.
Results may differ from the reference program's by a relative error of at most 0.00015.
Values sent between devices are 32-bit elements; how exact they have to be, the bound alone decides.
A program may use at most 128 MiB of HBM per device.

```python
import jax
import jax.numpy as jnp
from jax import lax

AXIAL = 1024
RANK = 128
R = 128
RJ = 16
RK = 16
ITERS = 2
J = 64
K = 32


def strengthened(result, rng, source, target, shards_of, factor):
    def block_of(axis_at):
        return (jnp.arange(result.shape[axis_at]) // (result.shape[axis_at] // shards_of)).reshape((-1,) + (1,) * (result.ndim - 1 - axis_at))

    first = jax.random.permutation(rng, shards_of)[block_of(target)]
    other_side = (block_of(target) + shards_of // 2) % shards_of
    return jnp.where((block_of(source) == first) | (block_of(source) == other_side), factor * result, result)


def steps_of(rng, dims, shards, low, largest):
    def one(axis_at, blocks):
        heights = jax.random.uniform(jax.random.fold_in(jax.random.fold_in(rng, 6), axis_at), (blocks,), jnp.float32, low / len(shards), largest / len(shards))
        return jnp.repeat(jnp.exp(heights), dims[axis_at] // blocks).reshape((-1,) + (1,) * (len(dims) - axis_at - 1))

    loudness = one(*shards[0])
    for cut in shards[1:]:
        loudness = loudness * one(*cut)
    return loudness


def centred(key, extent, spread, reach, cuts=(), dtype=jnp.bfloat16):
    loudness = steps_of(key, extent, cuts, -0.22, 0.18) if cuts else 1.0
    array = jax.random.normal(key, extent, jnp.float32) * spread * loudness
    return jnp.minimum(jnp.maximum(array, -reach), reach).astype(dtype)


def gaussian_with(stream_key, extent, width, reach, cuts, heavy, dtype=jnp.bfloat16):
    array = width * jax.random.normal(stream_key, extent, jnp.float32)
    if cuts:
        array = array * steps_of(stream_key, extent, cuts, -0.22, 0.18)
    return jnp.clip(strengthened(array, jax.random.fold_in(stream_key, 3), *heavy), -reach, reach).astype(dtype)


def setup_inputs(seed: int = 0) -> dict:
    streams_of = jax.random.split(jax.random.key(seed), 5)
    return {
        "tensor": centred(streams_of[0], (AXIAL, J, K, R), 1.0, 6.0, ((0, 2), (1, 16), (2, 8)), jnp.float32),
        "radial_factor": gaussian_with(streams_of[1], (J, RJ), J ** -0.5, 1.0, ((0, 16),), (0, 1, 16, 2.0), jnp.float32),
        "span_factor": gaussian_with(streams_of[2], (K, RK), K ** -0.5, 1.5, ((0, 8),), (0, 1, 8, 2.0), jnp.float32),
        "start_factor": centred(streams_of[3], (AXIAL, RANK), AXIAL ** -0.5, 0.1875, ((0, 2),), jnp.float32),
    }


def reference(tensor, radial_factor, span_factor, start_factor):
    highest = lax.Precision.HIGHEST
    radial_part = jnp.einsum('ijkr,jp->ipkr', tensor, radial_factor, precision=highest)
    projected = jnp.einsum('ipkr,kq->ipqr', radial_part, span_factor, precision=highest)
    unfolded = projected.reshape(AXIAL, RJ * RK * R)
    factor = start_factor
    for sweep_index in range(ITERS):
        small_matrix = jnp.dot(unfolded.T, factor, precision=highest)
        image_rows = jnp.dot(unfolded, small_matrix, precision=highest)
        gram_matrix = jnp.dot(image_rows.T, image_rows, precision=highest)
        cholesky_factor = jnp.linalg.cholesky(gram_matrix)
        factor = jax.scipy.linalg.solve_triangular(cholesky_factor, image_rows.T, lower=True).T
    core_block = jnp.dot(factor.T, unfolded, precision=highest)
    return core_block.reshape(RANK, RJ, RK, R)
```

```python
import functools

import jax
import jax.numpy as jnp
from jax import lax
from jax.experimental import pallas as pl
from jax.experimental.pallas import tpu as pltpu
from jax.sharding import PartitionSpec as P

MESH = pl.DeviceIdType.MESH
HIGHEST = lax.Precision.HIGHEST
LANES = 128
CHUNK = 8


def mm(a, b):
    return lax.dot_general(a, b, (((1,), (0,)), ((), ())), precision=HIGHEST, preferred_element_type=jnp.float32)


def mm_nt(a, b):
    return lax.dot_general(a, b, (((1,), (1,)), ((), ())), precision=HIGHEST, preferred_element_type=jnp.float32)


def mm_tn(a, b):
    return lax.dot_general(a, b, (((0,), (0,)), ((), ())), precision=HIGHEST, preferred_element_type=jnp.float32)


def iota(shape, dim):
    return lax.broadcasted_iota(jnp.int32, shape, dim)


def kernel(nr, nz, gx, t_ref, a_ref, b_ref, f_ref, out_ref,
           xb, ag, bg, ma, mb, ub, wb, ysend, yb, yt, f0t,
           sx, sr, part, r1, s1, r2, s2, im, gx_s, gr, ae, linv, cs, fr,
           own_sem, ab_send, ab_recv, t_send, t_recv, w_send, w_recv, y_send, y_recv,
           x_send, x_recv, g_send, g_recv, r1_send, r1_recv, r2_send, r2_recv, r3_send, r3_recv,
           f_send, f_recv):
    c = lax.axis_index("ax")
    m = lax.axis_index("rad")
    z = lax.axis_index("span")
    gy = nr // gx
    rj, rk = 2 * nz, nr
    il = f_ref.shape[0]
    bi = il // nr
    nc = bi // CHUNK
    my, mx = m // gx, m % gx

    def xy_peer(d):
        return ((my + d // gx) % gy) * gx + (mx + d % gx) % gx

    def z_peer(d):
        return (z + d) % nz

    def remote(src, dst, send, recv, dev):
        return pltpu.make_async_remote_copy(src_ref=src, dst_ref=dst, send_sem=send, recv_sem=recv, device_id=dev, device_id_type=MESH)

    def to_xy(src_of, dst, send, recv):
        @pl.loop(1, nr)
        def _(d):
            peer = xy_peer(d)
            remote(src_of(peer), dst, send, recv, (c, peer, z)).start()

    def to_z(src_of, dst, send, recv):
        @pl.loop(1, nz)
        def _(d):
            peer = z_peer(d)
            remote(src_of(peer), dst, send, recv, (c, m, peer)).start()

    def to_core(src, dst, send, recv):
        remote(src, dst, send, recv, (1 - c, m, z)).start()

    def wait(view, sem):
        pltpu.make_async_copy(view, view, sem).wait()

    dest_m, dest_z = 2 * z + c, m // 2
    src_c, src_z = m % 2, m // 2
    stays = jnp.logical_and(dest_m == m, dest_z == z)
    stays_here = jnp.logical_and(stays, src_c == c)

    barrier = pltpu.get_barrier_semaphore()

    def greet(dev):
        pl.semaphore_signal(barrier, inc=1, device_id=dev, device_id_type=MESH)

    @pl.loop(1, nr)
    def _(d):
        greet((c, xy_peer(d), z))

    @pl.loop(1, nz)
    def _(d):
        greet((c, m, z_peer(d)))

    greet((1 - c, m, z))
    for h in range(2):
        mine = jnp.logical_and(jnp.logical_and(src_c == c, 2 * z + h == m), src_z == z)

        @pl.when(jnp.logical_not(mine))
        def _():
            greet((src_c, 2 * z + h, src_z))

    ag[m] = jnp.zeros((8, LANES), jnp.float32)
    ag[m, 0:4, 0:rj] = a_ref[...]
    bg[z] = jnp.zeros((8, LANES), jnp.float32)
    bg[z, 0:4, 0:rk] = b_ref[...]
    pl.semaphore_wait(barrier, (nr - 1) + (nz - 1) + 1 + 2 - stays_here.astype(jnp.int32))

    to_xy(lambda p: ag.at[m], ag.at[m], ab_send.at[0], ab_recv.at[0])
    to_z(lambda p: bg.at[z], bg.at[z], ab_send.at[1], ab_recv.at[1])

    def t_rows(peer, k):
        return t_ref.at[pl.ds(pl.multiple_of((peer * bi + k * CHUNK) * 16, 128), CHUNK * 16), :]

    @pl.loop(0, nc)
    def _(k):
        pltpu.make_async_copy(t_rows(m, k), xb.at[k, m], own_sem.at[0, k]).start()
        to_xy(lambda p: t_rows(p, k), xb.at[k, m], t_send, t_recv.at[k])

    f0t[...] = f_ref[...].T

    wait(ag.at[pl.ds(0, nr - 1)], ab_recv.at[0])
    wait(bg.at[pl.ds(0, nz - 1)], ab_recv.at[1])

    rows, cols = rj * 4, nr * 16
    pick = (iota((rows, LANES), 0) // 4 == iota((rows, LANES), 1)).astype(jnp.float32)
    spread_row, spread_col = iota((nr * 8, cols), 0), iota((nr * 8, cols), 1)
    spread = (spread_row == (spread_col // 16) * 8 + (spread_col % 16) // 4).astype(jnp.float32)
    full = mm(mm_nt(pick, ag[...].reshape(nr * 8, LANES)), spread)
    ma[...] = jnp.where(iota((rows, cols), 0) % 4 == iota((rows, cols), 1) % 4, full, 0.0)

    rows, cols = rk * 16, nz * 64
    pick = (iota((rows, LANES), 0) // 16 == iota((rows, LANES), 1)).astype(jnp.float32)
    spread_row, spread_col = iota((nz * 8, cols), 0), iota((nz * 8, cols), 1)
    spread = (spread_row == (spread_col // 64) * 8 + spread_col % 4).astype(jnp.float32)
    full = mm(mm_nt(pick, bg[...].reshape(nz * 8, LANES)), spread)
    row, col = iota((rows, cols), 0), iota((rows, cols), 1)
    same = jnp.logical_and((row // 8) % 2 == (col // 4) % 2, row % 8 == (col // 8) % 8)
    mb[...] = jnp.where(same, full, 0.0)

    def radial(k):
        wait(xb.at[k, pl.ds(0, nr - 1)], t_recv.at[k])
        wait(xb.at[k, 0], own_sem.at[0, k])

        @pl.loop(0, CHUNK // 2)
        def _(h):
            at = pl.multiple_of(h * 32, 32)
            both = xb[k, :, pl.ds(at, 32), :]
            x0 = both[:, 0:16, :].reshape(nr * 16, LANES)
            x1 = both[:, 16:32, :].reshape(nr * 16, LANES)
            u = mm(ma[...], jnp.concatenate([x0, x1], axis=1))
            at8 = pl.multiple_of(h * 16, 16)
            ub[k, :, pl.ds(at8, 8), :] = u[:, 0:LANES].reshape(nz, 8, LANES)
            ub[k, :, pl.ds(at8 + 8, 8), :] = u[:, LANES:].reshape(nz, 8, LANES)

        pltpu.make_async_copy(ub.at[k, z], wb.at[k, z], own_sem.at[1, k]).start()
        to_z(lambda p: ub.at[k, p], wb.at[k, z], w_send, w_recv.at[k])

    def y_rows(k):
        return yb.at[:, pl.ds(pl.multiple_of(m * bi + k * CHUNK, 8), CHUNK), :]

    def span(k):
        wait(wb.at[k, pl.ds(0, nz - 1)], w_recv.at[k])
        wait(wb.at[k, 0], own_sem.at[1, k])
        y = mm(mb[...], wb[k].reshape(nz * 64, LANES))
        ysend[k] = y.reshape(nr, 2, CHUNK, LANES)
        pltpu.make_async_copy(ysend.at[k, m], y_rows(k), own_sem.at[2, k]).start()
        to_xy(lambda p: ysend.at[k, p], y_rows(k), y_send, y_recv)

    radial(0)

    @pl.loop(1, nc)
    def _(k):
        radial(k)
        span(k - 1)

    span(nc - 1)
    wait(yb.at[:, pl.ds(0, (nr - 1) * bi), :], y_recv)
    for k in range(nc):
        wait(ysend.at[0, 0], own_sem.at[2, k])

    def chol_start(gram):
        ae[:, 0:LANES] = gram
        eye = iota((LANES, LANES), 0) == iota((LANES, LANES), 1)
        ae[:, LANES:] = eye.astype(jnp.float32)

    sub = iota((8, LANES), 0)
    lane = iota((8, LANES), 1)

    def chol_blocks(lo, hi):
        @pl.loop(lo, hi)
        def _(b):
            at = pl.multiple_of(b * 8, 8)
            d = pltpu.roll(ae[pl.ds(at, 8), 0:LANES], (LANES - b * 8) % LANES, 1)
            e = ae[pl.ds(at, 8), LANES:]
            scale = jnp.zeros((8, LANES), jnp.float32)
            for t in range(8):
                column = jnp.broadcast_to(d[:, t:t + 1], (8, LANES))
                pivot = jnp.broadcast_to(column[t:t + 1, :], (8, LANES))
                f = jnp.where(sub > t, column / pivot, 0.0)
                scale = jnp.where(sub == t, lax.rsqrt(pivot), scale)
                d = d - f * jnp.broadcast_to(d[t:t + 1, :], (8, LANES))
                e = e - f * jnp.broadcast_to(e[t:t + 1, :], (8, LANES))
            d = pltpu.roll(d * scale, b * 8, 1)
            e = e * scale
            later = jnp.where(lane >= b * 8 + 8, d, 0.0)
            ae[...] -= mm_tn(later, jnp.concatenate([d, e], axis=1))
            ae[pl.ds(at, 8), LANES:] = e

    def exchange_begin(n):
        to_core(sx.at[n], sr.at[n], x_send.at[n], x_recv.at[n])

    def reduce_1(n):
        to_xy(lambda p: part.at[n, pl.ds(pl.multiple_of(p * bi, 8), bi), :], r1.at[n, m], r1_send.at[n], r1_recv.at[n])
        r1[n, m] = part[n, pl.ds(pl.multiple_of(m * bi, 8), bi), :]

    def reduce_2(n):
        wait(r1.at[n, pl.ds(0, nr - 1)], r1_recv.at[n])
        total = r1[n, 0]
        for k in range(1, nr):
            total = total + r1[n, k]
        s1[n] = total
        to_z(lambda p: s1.at[n], r2.at[n, z], r2_send.at[n], r2_recv.at[n])
        r2[n, z] = total

    def reduce_3(n):
        wait(r2.at[n, pl.ds(0, nz - 1)], r2_recv.at[n])
        total = r2[n, 0]
        for k in range(1, nz):
            total = total + r2[n, k]
        s2[n] = total
        mine = pl.ds(pl.multiple_of(m * bi, 8), bi)
        to_xy(lambda p: s2.at[n], im.at[n, mine, :], r3_send.at[n], r3_recv.at[n])
        im[n, mine, :] = total

    def reduce_end(n):
        wait(im.at[n, pl.ds(0, (nr - 1) * bi), :], r3_recv.at[n])

    for p in range(2):
        sx[0, p] = mm(f0t[...], yb[p])
    exchange_begin(0)
    wait(sr.at[0], x_recv.at[0])
    part[0] = mm_nt(yb[0], sx[0, 0] + sr[0, 0]) + mm_nt(yb[1], sx[0, 1] + sr[0, 1])
    reduce_1(0)
    yt[0] = yb[0].T
    reduce_2(0)
    yt[1] = yb[1].T
    reduce_3(0)
    reduce_end(0)

    for p in range(2):
        sx[1, p] = mm(yt[p], im[0])
    exchange_begin(1)
    gx_s[0] = mm(im[0].T, im[0])
    to_core(gx_s.at[0], gr.at[0], g_send.at[0], g_recv.at[0])
    wait(sr.at[1], x_recv.at[1])
    part[1] = mm(yb[0], sx[1, 0] + sr[1, 0]) + mm(yb[1], sx[1, 1] + sr[1, 1])
    reduce_1(1)
    blocks = LANES // 8
    wait(gr.at[0], g_recv.at[0])
    chol_start(gx_s[0] + gr[0])
    chol_blocks(0, 5)
    reduce_2(1)
    chol_blocks(5, 10)
    reduce_3(1)
    chol_blocks(10, blocks)
    linv[...] = ae[:, LANES:]
    reduce_end(1)
    images = mm_nt(im[1], linv[...])
    gx_s[1] = mm(images.T, images)
    to_core(gx_s.at[1], gr.at[1], g_send.at[1], g_recv.at[1])

    for p in range(2):
        sx[2, p] = mm(yt[p], images)
    to_core(sx.at[2, 1 - c], sr.at[2, 0], x_send.at[2], x_recv.at[2])
    wait(gr.at[1], g_recv.at[1])
    chol_start(gx_s[1] + gr[1])
    chol_blocks(0, 3)
    wait(sr.at[2, 0], x_recv.at[2])
    cs[...] = sx[2, c] + sr[2, 0]
    slot = m % 2
    for h in range(2):
        @pl.when(jnp.logical_and(stays, c == h))
        def _():
            pltpu.make_async_copy(cs, fr.at[slot], f_recv.at[slot]).start()

        @pl.when(jnp.logical_not(jnp.logical_and(stays, c == h)))
        def _():
            remote(cs, fr.at[slot], f_send.at[h], f_recv.at[slot], (h, dest_m, dest_z)).start()

    chol_blocks(3, blocks)
    for q in range(2):
        wait(fr.at[q], f_recv.at[q])
        out_ref[:, q, :] = mm_nt(ae[:, LANES:], fr[q])

    wait(ag.at[pl.ds(0, nr - 1)], ab_send.at[0])
    wait(bg.at[pl.ds(0, nz - 1)], ab_send.at[1])
    wait(xb.at[:, pl.ds(0, nr - 1)], t_send)
    wait(wb.at[:, pl.ds(0, nz - 1)], w_send)
    wait(ysend.at[:, pl.ds(0, nr - 1)], y_send)
    for n in range(2):
        wait(sr.at[n], x_send.at[n])
        wait(gr.at[n], g_send.at[n])
        wait(r1.at[n, pl.ds(0, nr - 1)], r1_send.at[n])
        wait(r2.at[n, pl.ds(0, nz - 1)], r2_send.at[n])
        wait(im.at[n, pl.ds(0, (nr - 1) * bi), :], r3_send.at[n])
    wait(sr.at[2, 0], x_send.at[2])
    for h in range(2):
        @pl.when(jnp.logical_not(jnp.logical_and(stays, c == h)))
        def _():
            wait(cs, f_send.at[h])


def solution(mesh):
    nr, nz = mesh.shape["rad"], mesh.shape["span"]
    gx = 1
    while gx * gx < nr:
        gx *= 2

    def body(tensor, radial_factor, span_factor, start_factor):
        il = start_factor.shape[0]
        bi = il // nr
        nc = bi // CHUNK
        f32 = jnp.float32
        dma = pltpu.SemaphoreType.DMA
        vm = lambda *s: pltpu.VMEM(s, f32)
        scratch = [
            vm(nc, nr, CHUNK * 16, LANES),
            vm(nr, 8, LANES), vm(nz, 8, LANES),
            vm(nz * 8, nr * 16), vm(nr * 16, nz * 64),
            vm(nc, nz, CHUNK * 8, LANES), vm(nc, nz, CHUNK * 8, LANES),
            vm(nc, nr, 2, CHUNK, LANES),
            vm(2, il, LANES), vm(2, LANES, il), vm(LANES, il),
            vm(3, 2, LANES, LANES), vm(3, 2, LANES, LANES),
            vm(2, il, LANES),
            vm(2, nr, bi, LANES), vm(2, bi, LANES),
            vm(2, nz, bi, LANES), vm(2, bi, LANES),
            vm(2, il, LANES),
            vm(2, LANES, LANES), vm(2, LANES, LANES),
            vm(LANES, 2 * LANES), vm(LANES, LANES),
            vm(LANES, LANES), vm(2, LANES, LANES),
            dma((3, nc)),
            dma((2,)), dma((2,)),
            dma, dma((nc,)),
            dma, dma((nc,)),
            dma, dma,
            dma((3,)), dma((3,)),
            dma((2,)), dma((2,)),
            dma((2,)), dma((2,)), dma((2,)), dma((2,)), dma((2,)), dma((2,)),
            dma((2,)), dma((2,)),
        ]
        rows = tensor.reshape(il * 16, LANES)
        vmem = pl.BlockSpec(memory_space=pltpu.VMEM)
        core = pl.pallas_call(
            functools.partial(kernel, nr, nz, gx),
            out_shape=jax.ShapeDtypeStruct((LANES, 2, LANES), f32),
            in_specs=[pl.BlockSpec(memory_space=pl.ANY), vmem, vmem, vmem],
            out_specs=vmem,
            scratch_shapes=scratch,
            compiler_params=pltpu.CompilerParams(collective_id=0, has_side_effects=True, vmem_limit_bytes=48 * 1024 * 1024),
        )(rows, radial_factor, span_factor, start_factor)
        return core.reshape(LANES, 1, 2, LANES)

    in_specs = (P("ax", "rad", "span", None), P("rad", None), P("span", None), P("ax", None))
    out_specs = P(None, "rad", "span", None)
    return jax.shard_map(body, mesh=mesh, in_specs=in_specs, out_specs=out_specs, check_vma=False)
```

```python
import functools

import jax
import jax.numpy as jnp
from jax import lax
from jax.experimental import pallas as pl
from jax.experimental.pallas import tpu as pltpu
from jax.sharding import PartitionSpec as P

MESH = pl.DeviceIdType.MESH
HIGHEST = lax.Precision.HIGHEST
LANES = 128
CHUNK = 4
GROUP = 8
PIVOTS = 16


def mm(a, b):
    return lax.dot_general(a, b, (((1,), (0,)), ((), ())), precision=HIGHEST, preferred_element_type=jnp.float32)


def mm_nt(a, b):
    return lax.dot_general(a, b, (((1,), (1,)), ((), ())), precision=HIGHEST, preferred_element_type=jnp.float32)


def mm_tn(a, b):
    return lax.dot_general(a, b, (((0,), (0,)), ((), ())), precision=HIGHEST, preferred_element_type=jnp.float32)


def split3(x):
    high = x.astype(jnp.bfloat16)
    rest = x - high.astype(jnp.float32)
    mid = rest.astype(jnp.bfloat16)
    return high, mid, (rest - mid.astype(jnp.float32)).astype(jnp.bfloat16)


def mm_tn_stacked(a, b):
    ah, am, al = split3(a)
    bh, bm, bl = split3(b)
    left = jnp.concatenate([ah, ah, ah, am, am, al], axis=0)
    right = jnp.concatenate([bh, bm, bl, bh, bm, bh], axis=0)
    return lax.dot_general(left, right, (((0,), (0,)), ((), ())), preferred_element_type=jnp.float32)


def iota(shape, dim):
    return lax.broadcasted_iota(jnp.int32, shape, dim)


def kernel(nr, nz, gx, t_ref, a_ref, b_ref, f_ref, out_ref,
           av, bv, fv, xb, ag, bg, ma, mb, ub, wb, ysend, yb, yt, f0t,
           sx, sr, part, r1, s1, r2, s2, im, gx_s, gr, ae, linv, cs, fr,
           in_sem, own_sem, ab_send, ab_recv, t_send, t_recv, w_send, w_recv, y_send, y_recv,
           x_send, x_recv, g_send, g_recv, r1_send, r1_recv, r2_send, r2_recv, r3_send, r3_recv,
           f_send, f_recv):
    c = lax.axis_index("ax")
    m = lax.axis_index("rad")
    z = lax.axis_index("span")
    gy = nr // gx
    rj, rk = 2 * nz, nr
    il = f_ref.shape[0]
    bi = il // nr
    nc, ng, per = bi // CHUNK, bi // GROUP, GROUP // CHUNK
    my, mx = m // gx, m % gx

    def xy_peer(d):
        return ((my + d // gx) % gy) * gx + (mx + d % gx) % gx

    def z_peer(d):
        return (z + d) % nz

    def remote(src, dst, send, recv, dev):
        return pltpu.make_async_remote_copy(src_ref=src, dst_ref=dst, send_sem=send, recv_sem=recv, device_id=dev, device_id_type=MESH)

    def to_xy(src_of, dst, send, recv):
        @pl.loop(1, nr)
        def _(d):
            peer = xy_peer(d)
            remote(src_of(peer), dst, send, recv, (c, peer, z)).start()

    def to_z(src_of, dst, send, recv):
        @pl.loop(1, nz)
        def _(d):
            peer = z_peer(d)
            remote(src_of(peer), dst, send, recv, (c, m, peer)).start()

    def to_core(src, dst, send, recv):
        remote(src, dst, send, recv, (1 - c, m, z)).start()

    def wait(view, sem):
        pltpu.make_async_copy(view, view, sem).wait()

    pending = []

    def finish():
        for view, sem in pending:
            wait(view, sem)

    dest_m, dest_z = 2 * z + c, m // 2
    src_c, src_z = m % 2, m // 2
    stays = jnp.logical_and(dest_m == m, dest_z == z)
    stays_here = jnp.logical_and(stays, src_c == c)

    arriving = [pltpu.make_async_copy(src, dst, in_sem.at[n]) for n, (src, dst) in enumerate(((a_ref, av), (b_ref, bv), (f_ref, fv)))]
    for copy in arriving:
        copy.start()

    barrier = pltpu.get_barrier_semaphore()

    def greet(dev):
        pl.semaphore_signal(barrier, inc=1, device_id=dev, device_id_type=MESH)

    @pl.loop(1, nr)
    def _(d):
        greet((c, xy_peer(d), z))

    @pl.loop(1, nz)
    def _(d):
        greet((c, m, z_peer(d)))

    greet((1 - c, m, z))
    for h in range(2):
        mine = jnp.logical_and(jnp.logical_and(src_c == c, 2 * z + h == m), src_z == z)

        @pl.when(jnp.logical_not(mine))
        def _():
            greet((src_c, 2 * z + h, src_z))

    arriving[0].wait()
    arriving[1].wait()
    ag[m] = jnp.zeros((8, LANES), jnp.float32)
    ag[m, 0:4, 0:rj] = av[...]
    bg[z] = jnp.zeros((8, LANES), jnp.float32)
    bg[z, 0:4, 0:rk] = bv[...]
    pl.semaphore_wait(barrier, (nr - 1) + (nz - 1) + 1 + 2 - stays_here.astype(jnp.int32))

    to_xy(lambda p: ag.at[m], ag.at[m], ab_send.at[0], ab_recv.at[0])
    pending.append((ag.at[pl.ds(0, nr - 1)], ab_send.at[0]))
    to_z(lambda p: bg.at[z], bg.at[z], ab_send.at[1], ab_recv.at[1])
    pending.append((bg.at[pl.ds(0, nz - 1)], ab_send.at[1]))

    def t_rows(peer, k):
        return t_ref.at[pl.ds(pl.multiple_of((peer * bi + k * CHUNK) * 16, 64), CHUNK * 16), :]

    @pl.loop(0, nc)
    def _(k):
        pltpu.make_async_copy(t_rows(m, k), xb.at[k, m], own_sem.at[0, k]).start()
        to_xy(lambda p: t_rows(p, k), xb.at[k, m], t_send, t_recv.at[k])

    pending.append((xb.at[:, pl.ds(0, nr - 1)], t_send))
    arriving[2].wait()
    f0t[...] = fv[...].T

    wait(ag.at[pl.ds(0, nr - 1)], ab_recv.at[0])
    wait(bg.at[pl.ds(0, nz - 1)], ab_recv.at[1])

    rows, cols = rj * 4, nr * 16
    pick = (iota((rows, LANES), 0) // 4 == iota((rows, LANES), 1)).astype(jnp.float32)
    spread_row, spread_col = iota((nr * 8, cols), 0), iota((nr * 8, cols), 1)
    spread = (spread_row == (spread_col // 16) * 8 + (spread_col % 16) // 4).astype(jnp.float32)
    full = mm(mm_nt(pick, ag[...].reshape(nr * 8, LANES)), spread)
    ma[...] = jnp.where(iota((rows, cols), 0) % 4 == iota((rows, cols), 1) % 4, full, 0.0)

    rows, cols = rk * 16, nz * 64
    pick = (iota((rows, LANES), 0) // 16 == iota((rows, LANES), 1)).astype(jnp.float32)
    spread_row, spread_col = iota((nz * 8, cols), 0), iota((nz * 8, cols), 1)
    spread = (spread_row == (spread_col // 64) * 8 + spread_col % 4).astype(jnp.float32)
    full = mm(mm_nt(pick, bg[...].reshape(nz * 8, LANES)), spread)
    row, col = iota((rows, cols), 0), iota((rows, cols), 1)
    same = jnp.logical_and((row // 8) % 2 == (col // 4) % 2, row % 8 == (col // 8) % 8)
    mb[...] = jnp.where(same, full, 0.0)

    def radial(k):
        wait(xb.at[k, pl.ds(0, nr - 1)], t_recv.at[k])
        wait(xb.at[k, 0], own_sem.at[0, k])

        @pl.loop(0, CHUNK // 2)
        def _(h):
            at = pl.multiple_of(h * 32, 32)
            both = xb[k, :, pl.ds(at, 32), :]
            x0 = both[:, 0:16, :].reshape(nr * 16, LANES)
            x1 = both[:, 16:32, :].reshape(nr * 16, LANES)
            u = mm(ma[...], jnp.concatenate([x0, x1], axis=1))
            at8 = pl.multiple_of((k % per) * CHUNK * 8 + h * 16, 16)
            ub[k // per, :, pl.ds(at8, 8), :] = u[:, 0:LANES].reshape(nz, 8, LANES)
            ub[k // per, :, pl.ds(at8 + 8, 8), :] = u[:, LANES:].reshape(nz, 8, LANES)

        g, half = k // per, pl.ds(pl.multiple_of((k % per) * CHUNK * 8, CHUNK * 8), CHUNK * 8)
        pltpu.make_async_copy(ub.at[g, z, half], wb.at[g, z, half], own_sem.at[1, k]).start()
        to_z(lambda p: ub.at[g, p, half], wb.at[g, z, half], w_send, w_recv.at[k])

    def y_rows(g):
        return yb.at[:, pl.ds(pl.multiple_of(m * bi + g * GROUP, 8), GROUP), :]

    def span(g):
        for h in range(per):
            wait(wb.at[g, pl.ds(0, nz - 1), pl.ds(0, CHUNK * 8)], w_recv.at[g * per + h])
            wait(wb.at[g, 0, pl.ds(0, CHUNK * 8)], own_sem.at[1, g * per + h])
        y = mm(mb[...], wb[g].reshape(nz * 64, LANES))
        ysend[g] = y.reshape(nr, 2, GROUP, LANES)
        pltpu.make_async_copy(ysend.at[g, m], y_rows(g), own_sem.at[2, g]).start()
        to_xy(lambda p: ysend.at[g, p], y_rows(g), y_send, y_recv)

    radial(0)
    radial(1)

    @pl.loop(1, ng)
    def _(g):
        radial(g * per)
        span(g - 1)
        radial(g * per + 1)

    span(ng - 1)
    pending.extend([(wb.at[:, pl.ds(0, nz - 1)], w_send), (ysend.at[:, pl.ds(0, nr - 1)], y_send)])
    wait(yb.at[:, pl.ds(0, (nr - 1) * bi), :], y_recv)
    for g in range(ng):
        wait(ysend.at[0, 0], own_sem.at[2, g])

    def chol_start(gram):
        ae[:, 0:LANES] = gram
        eye = iota((LANES, LANES), 0) == iota((LANES, LANES), 1)
        ae[:, LANES:] = eye.astype(jnp.float32)

    tiles = range(PIVOTS // 8)
    sub = [iota((8, LANES), 0) + 8 * g for g in tiles]
    lane = iota((PIVOTS, LANES), 1)

    def over_rows(x, t):
        return jnp.broadcast_to(x[t:t + 1, :], (8, LANES))

    def chol_blocks(lo, hi):
        @pl.loop(lo, hi)
        def _(b):
            at = pl.multiple_of(b * PIVOTS, PIVOTS)
            turned = pltpu.roll(ae[pl.ds(at, PIVOTS), 0:LANES], (LANES - b * PIVOTS) % LANES, 1)
            d = [turned[8 * g:8 * g + 8] for g in tiles]
            e = [ae[pl.ds(at + 8 * g, 8), LANES:] for g in tiles]
            cols = [[jnp.broadcast_to(d[g][:, t:t + 1], (8, LANES)) for g in tiles] for t in range(PIVOTS)]
            scale = [jnp.zeros((8, LANES), jnp.float32) for g in tiles]
            for t in range(PIVOTS):
                g0, t0 = t // 8, t % 8
                pivot = over_rows(cols[t][g0], t0)
                r = pltpu.reciprocal(pivot, approx=True)
                r = r * (2.0 - pivot * r)
                r = r * (2.0 - pivot * r)
                f = {g: cols[t][g] * r for g in tiles if g >= g0}
                f[g0] = jnp.where(sub[g0] > t, f[g0], 0.0)
                scale[g0] = jnp.where(sub[g0] == t, lax.rsqrt(pivot), scale[g0])
                for u in range(t + 1, PIVOTS):
                    row = over_rows(cols[u][g0], t0)
                    for g in f:
                        cols[u][g] = cols[u][g] - f[g] * row
                d_row, e_row = over_rows(d[g0], t0), over_rows(e[g0], t0)
                for g in f:
                    d[g] = d[g] - f[g] * d_row
                    e[g] = e[g] - f[g] * e_row
            rows = pltpu.roll(jnp.concatenate([d[g] * scale[g] for g in tiles], axis=0), b * PIVOTS, 1)
            inverse = jnp.concatenate([e[g] * scale[g] for g in tiles], axis=0)
            later = jnp.where(lane >= b * PIVOTS + PIVOTS, rows, 0.0)
            ae[...] -= mm_tn_stacked(later, jnp.concatenate([rows, inverse], axis=1))
            ae[pl.ds(at, PIVOTS), LANES:] = inverse

    def exchange_begin(n):
        to_core(sx.at[n], sr.at[n], x_send.at[n], x_recv.at[n])
        pending.append((sr.at[n], x_send.at[n]))

    def reduce_1(n):
        to_xy(lambda p: part.at[n, pl.ds(pl.multiple_of(p * bi, 8), bi), :], r1.at[n, m], r1_send.at[n], r1_recv.at[n])
        pending.append((r1.at[n, pl.ds(0, nr - 1)], r1_send.at[n]))
        r1[n, m] = part[n, pl.ds(pl.multiple_of(m * bi, 8), bi), :]

    def reduce_2(n):
        wait(r1.at[n, pl.ds(0, nr - 1)], r1_recv.at[n])
        total = r1[n, 0]
        for k in range(1, nr):
            total = total + r1[n, k]
        s1[n] = total
        to_z(lambda p: s1.at[n], r2.at[n, z], r2_send.at[n], r2_recv.at[n])
        pending.append((r2.at[n, pl.ds(0, nz - 1)], r2_send.at[n]))
        r2[n, z] = total

    def reduce_3(n):
        wait(r2.at[n, pl.ds(0, nz - 1)], r2_recv.at[n])
        total = r2[n, 0]
        for k in range(1, nz):
            total = total + r2[n, k]
        s2[n] = total
        mine = pl.ds(pl.multiple_of(m * bi, 8), bi)
        to_xy(lambda p: s2.at[n], im.at[n, mine, :], r3_send.at[n], r3_recv.at[n])
        pending.append((im.at[n, pl.ds(0, (nr - 1) * bi), :], r3_send.at[n]))
        im[n, mine, :] = total

    def reduce_end(n):
        wait(im.at[n, pl.ds(0, (nr - 1) * bi), :], r3_recv.at[n])

    for p in range(2):
        sx[0, p] = mm(f0t[...], yb[p])
    exchange_begin(0)
    wait(sr.at[0], x_recv.at[0])
    part[0] = mm_nt(yb[0], sx[0, 0] + sr[0, 0]) + mm_nt(yb[1], sx[0, 1] + sr[0, 1])
    reduce_1(0)
    yt[0] = yb[0].T
    reduce_2(0)
    yt[1] = yb[1].T
    reduce_3(0)
    reduce_end(0)

    for p in range(2):
        sx[1, p] = mm(yt[p], im[0])
    exchange_begin(1)
    gx_s[0] = mm(im[0].T, im[0])
    to_core(gx_s.at[0], gr.at[0], g_send.at[0], g_recv.at[0])
    pending.append((gr.at[0], g_send.at[0]))
    wait(sr.at[1], x_recv.at[1])
    part[1] = mm(yb[0], sx[1, 0] + sr[1, 0]) + mm(yb[1], sx[1, 1] + sr[1, 1])
    reduce_1(1)
    blocks = LANES // PIVOTS
    wait(gr.at[0], g_recv.at[0])
    chol_start(gx_s[0] + gr[0])
    chol_blocks(0, 3)
    reduce_2(1)
    chol_blocks(3, 6)
    reduce_3(1)
    chol_blocks(6, blocks)
    linv[...] = ae[:, LANES:]
    reduce_end(1)
    images = mm_nt(im[1], linv[...])
    gx_s[1] = mm(images.T, images)
    to_core(gx_s.at[1], gr.at[1], g_send.at[1], g_recv.at[1])
    pending.append((gr.at[1], g_send.at[1]))

    for p in range(2):
        sx[2, p] = mm(yt[p], images)
    to_core(sx.at[2, 1 - c], sr.at[2, 0], x_send.at[2], x_recv.at[2])
    pending.append((sr.at[2, 0], x_send.at[2]))
    wait(gr.at[1], g_recv.at[1])
    chol_start(gx_s[1] + gr[1])
    chol_blocks(0, 2)
    wait(sr.at[2, 0], x_recv.at[2])
    cs[...] = sx[2, c] + sr[2, 0]
    slot = m % 2
    for h in range(2):
        @pl.when(jnp.logical_and(stays, c == h))
        def _():
            pltpu.make_async_copy(cs, fr.at[slot], f_recv.at[slot]).start()

        @pl.when(jnp.logical_not(jnp.logical_and(stays, c == h)))
        def _():
            remote(cs, fr.at[slot], f_send.at[h], f_recv.at[slot], (h, dest_m, dest_z)).start()

    chol_blocks(2, blocks)
    for q in range(2):
        wait(fr.at[q], f_recv.at[q])
        out_ref[:, q, :] = mm_nt(ae[:, LANES:], fr[q])

    finish()
    for h in range(2):
        @pl.when(jnp.logical_not(jnp.logical_and(stays, c == h)))
        def _():
            wait(cs, f_send.at[h])


def solution(mesh):
    nr, nz = mesh.shape["rad"], mesh.shape["span"]
    gx = 1
    while gx * gx < nr:
        gx *= 2

    def body(tensor, radial_factor, span_factor, start_factor):
        il = start_factor.shape[0]
        bi = il // nr
        nc, ng = bi // CHUNK, bi // GROUP
        f32 = jnp.float32
        dma = pltpu.SemaphoreType.DMA
        vm = lambda *s: pltpu.VMEM(s, f32)
        scratch = [
            vm(*radial_factor.shape), vm(*span_factor.shape), vm(*start_factor.shape),
            vm(nc, nr, CHUNK * 16, LANES),
            vm(nr, 8, LANES), vm(nz, 8, LANES),
            vm(nz * 8, nr * 16), vm(nr * 16, nz * 64),
            vm(ng, nz, GROUP * 8, LANES), vm(ng, nz, GROUP * 8, LANES),
            vm(ng, nr, 2, GROUP, LANES),
            vm(2, il, LANES), vm(2, LANES, il), vm(LANES, il),
            vm(3, 2, LANES, LANES), vm(3, 2, LANES, LANES),
            vm(2, il, LANES),
            vm(2, nr, bi, LANES), vm(2, bi, LANES),
            vm(2, nz, bi, LANES), vm(2, bi, LANES),
            vm(2, il, LANES),
            vm(2, LANES, LANES), vm(2, LANES, LANES),
            vm(LANES, 2 * LANES), vm(LANES, LANES),
            vm(LANES, LANES), vm(2, LANES, LANES),
            dma((3,)), dma((3, nc)),
            dma((2,)), dma((2,)),
            dma, dma((nc,)),
            dma, dma((nc,)),
            dma, dma,
            dma((3,)), dma((3,)),
            dma((2,)), dma((2,)),
            dma((2,)), dma((2,)), dma((2,)), dma((2,)), dma((2,)), dma((2,)),
            dma((2,)), dma((2,)),
        ]
        rows = tensor.reshape(il * 16, LANES)
        hbm = pl.BlockSpec(memory_space=pltpu.HBM)
        core = pl.pallas_call(
            functools.partial(kernel, nr, nz, gx),
            out_shape=jax.ShapeDtypeStruct((LANES, 2, LANES), f32),
            in_specs=[hbm] * 4,
            out_specs=pl.BlockSpec(memory_space=pltpu.VMEM),
            scratch_shapes=scratch,
            compiler_params=pltpu.CompilerParams(collective_id=0, has_side_effects=True, vmem_limit_bytes=62 * 1024 * 1024),
        )(rows, radial_factor, span_factor, start_factor)
        return core.reshape(LANES, 1, 2, LANES)

    in_specs = (P("ax", "rad", "span", None), P("rad", None), P("span", None), P("ax", None))
    out_specs = P(None, "rad", "span", None)
    return jax.shard_map(body, mesh=mesh, in_specs=in_specs, out_specs=out_specs, check_vma=False)
```

```python
import functools

import jax
import jax.numpy as jnp
from jax import lax
from jax.experimental import pallas as pl
from jax.experimental.pallas import tpu as pltpu
from jax.sharding import PartitionSpec as P

MESH = pl.DeviceIdType.MESH
HIGHEST = lax.Precision.HIGHEST
LANES = 128
CHUNK = 4
GROUP = 8
PIVOTS = 16


def mm(a, b):
    return lax.dot_general(a, b, (((1,), (0,)), ((), ())), precision=HIGHEST, preferred_element_type=jnp.float32)


def mm_nt(a, b):
    return lax.dot_general(a, b, (((1,), (1,)), ((), ())), precision=HIGHEST, preferred_element_type=jnp.float32)


def mm_tn(a, b):
    return lax.dot_general(a, b, (((0,), (0,)), ((), ())), precision=HIGHEST, preferred_element_type=jnp.float32)


def split3(x):
    high = x.astype(jnp.bfloat16)
    rest = x - high.astype(jnp.float32)
    mid = rest.astype(jnp.bfloat16)
    return high, mid, (rest - mid.astype(jnp.float32)).astype(jnp.bfloat16)


def mm_tn_stacked(a, b):
    ah, am, al = split3(a)
    bh, bm, bl = split3(b)
    left = jnp.concatenate([ah, ah, ah, am, am, al], axis=0)
    right = jnp.concatenate([bh, bm, bl, bh, bm, bh], axis=0)
    return lax.dot_general(left, right, (((0,), (0,)), ((), ())), preferred_element_type=jnp.float32)


def iota(shape, dim):
    return lax.broadcasted_iota(jnp.int32, shape, dim)


def kernel(nr, nz, gx, t_ref, a_ref, b_ref, f_ref, out_ref,
           av, bv, fv, xb, ag, bg, ma, mb, ub, wb, ysend, yb, yt, f0t,
           sx, sr, part, r1, s1, r2, s2, im, gx_s, gr, ae, linv, ya, yo, yot,
           in_sem, own_sem, ab_send, ab_recv, t_send, t_recv, w_send, w_recv, y_send, y_recv,
           x_send, x_recv, g_send, g_recv, r1_send, r1_recv, r2_send, r2_recv, r3_send, r3_recv,
           v_send, v_recv):
    c = lax.axis_index("ax")
    m = lax.axis_index("rad")
    z = lax.axis_index("span")
    gy = nr // gx
    rj, rk = 2 * nz, nr
    il = f_ref.shape[0]
    bi = il // nr
    nc, ng, per = bi // CHUNK, bi // GROUP, GROUP // CHUNK
    my, mx = m // gx, m % gx

    def xy_peer(d):
        return lax.rem(my + lax.div(d, gx), gy) * gx + lax.rem(mx + lax.rem(d, gx), gx)

    def z_peer(d):
        return lax.rem(z + d, nz)

    def remote(src, dst, send, recv, dev):
        return pltpu.make_async_remote_copy(src_ref=src, dst_ref=dst, send_sem=send, recv_sem=recv, device_id=dev, device_id_type=MESH)

    def to_xy(src_of, dst, send, recv):
        @pl.loop(1, nr)
        def _(d):
            peer = xy_peer(d)
            remote(src_of(peer), dst, send, recv, (c, peer, z)).start()

    def to_z(src_of, dst, send, recv):
        @pl.loop(1, nz)
        def _(d):
            peer = z_peer(d)
            remote(src_of(peer), dst, send, recv, (c, m, peer)).start()

    def to_core(src, dst, send, recv):
        remote(src, dst, send, recv, (1 - c, m, z)).start()

    def wait(view, sem):
        pltpu.make_async_copy(view, view, sem).wait()

    pending = []

    def finish():
        for view, sem in pending:
            wait(view, sem)

    arriving = [pltpu.make_async_copy(src, dst, in_sem.at[n]) for n, (src, dst) in enumerate(((a_ref, av), (b_ref, bv), (f_ref, fv)))]
    for copy in arriving:
        copy.start()

    barrier = pltpu.get_barrier_semaphore()

    def greet(dev):
        pl.semaphore_signal(barrier, inc=1, device_id=dev, device_id_type=MESH)

    @pl.loop(1, nr)
    def _(d):
        greet((c, xy_peer(d), z))

    @pl.loop(1, nz)
    def _(d):
        greet((c, m, z_peer(d)))

    greet((1 - c, m, z))
    arriving[0].wait()
    arriving[1].wait()
    ag[m] = jnp.zeros((8, LANES), jnp.float32)
    ag[m, 0:4, 0:rj] = av[...]
    bg[z] = jnp.zeros((8, LANES), jnp.float32)
    bg[z, 0:4, 0:rk] = bv[...]
    pl.semaphore_wait(barrier, (nr - 1) + (nz - 1) + 1)

    to_xy(lambda p: ag.at[m], ag.at[m], ab_send.at[0], ab_recv.at[0])
    pending.append((ag.at[pl.ds(0, nr - 1)], ab_send.at[0]))
    to_z(lambda p: bg.at[z], bg.at[z], ab_send.at[1], ab_recv.at[1])
    pending.append((bg.at[pl.ds(0, nz - 1)], ab_send.at[1]))

    def t_rows(peer, k):
        return t_ref.at[pl.ds(pl.multiple_of((peer * bi + k * CHUNK) * 16, 64), CHUNK * 16), :]

    @pl.loop(0, nc)
    def _(k):
        pltpu.make_async_copy(t_rows(m, k), xb.at[k, m], own_sem.at[0, k]).start()
        to_xy(lambda p: t_rows(p, k), xb.at[k, m], t_send, t_recv.at[k])

    pending.append((xb.at[:, pl.ds(0, nr - 1)], t_send))
    arriving[2].wait()
    f0t[...] = fv[...].T

    wait(ag.at[pl.ds(0, nr - 1)], ab_recv.at[0])
    wait(bg.at[pl.ds(0, nz - 1)], ab_recv.at[1])

    rows, cols = rj * 4, nr * 16
    pick = (iota((rows, LANES), 0) // 4 == iota((rows, LANES), 1)).astype(jnp.float32)
    spread_row, spread_col = iota((nr * 8, cols), 0), iota((nr * 8, cols), 1)
    spread = (spread_row == (spread_col // 16) * 8 + (spread_col % 16) // 4).astype(jnp.float32)
    full = mm(mm_nt(pick, ag[...].reshape(nr * 8, LANES)), spread)
    ma[...] = jnp.where(iota((rows, cols), 0) % 4 == iota((rows, cols), 1) % 4, full, 0.0)

    rows, cols = rk * 16, nz * 64
    pick = (iota((rows, LANES), 0) // 16 == iota((rows, LANES), 1)).astype(jnp.float32)
    spread_row, spread_col = iota((nz * 8, cols), 0), iota((nz * 8, cols), 1)
    spread = (spread_row == (spread_col // 64) * 8 + spread_col % 4).astype(jnp.float32)
    full = mm(mm_nt(pick, bg[...].reshape(nz * 8, LANES)), spread)
    row, col = iota((rows, cols), 0), iota((rows, cols), 1)
    same = jnp.logical_and((row // 8) % 2 == (col // 4) % 2, row % 8 == (col // 8) % 8)
    mb[...] = jnp.where(same, full, 0.0)

    def radial(k):
        wait(xb.at[k, pl.ds(0, nr - 1)], t_recv.at[k])
        wait(xb.at[k, 0], own_sem.at[0, k])

        @pl.loop(0, CHUNK // 2)
        def _(h):
            at = pl.multiple_of(h * 32, 32)
            both = xb[k, :, pl.ds(at, 32), :]
            x0 = both[:, 0:16, :].reshape(nr * 16, LANES)
            x1 = both[:, 16:32, :].reshape(nr * 16, LANES)
            u = mm(ma[...], jnp.concatenate([x0, x1], axis=1))
            at8 = pl.multiple_of((k % per) * CHUNK * 8 + h * 16, 16)
            ub[k // per, :, pl.ds(at8, 8), :] = u[:, 0:LANES].reshape(nz, 8, LANES)
            ub[k // per, :, pl.ds(at8 + 8, 8), :] = u[:, LANES:].reshape(nz, 8, LANES)

        g, half = k // per, pl.ds(pl.multiple_of((k % per) * CHUNK * 8, CHUNK * 8), CHUNK * 8)
        pltpu.make_async_copy(ub.at[g, z, half], wb.at[g, z, half], own_sem.at[1, k]).start()
        to_z(lambda p: ub.at[g, p, half], wb.at[g, z, half], w_send, w_recv.at[k])

    def y_rows(g):
        return yb.at[:, pl.ds(pl.multiple_of(m * bi + g * GROUP, 8), GROUP), :]

    def span(g):
        for h in range(per):
            wait(wb.at[g, pl.ds(0, nz - 1), pl.ds(0, CHUNK * 8)], w_recv.at[g * per + h])
            wait(wb.at[g, 0, pl.ds(0, CHUNK * 8)], own_sem.at[1, g * per + h])
        y = mm(mb[...], wb[g].reshape(nz * 64, LANES))
        ysend[g] = y.reshape(nr, 2, GROUP, LANES)
        pltpu.make_async_copy(ysend.at[g, m], y_rows(g), own_sem.at[2, g]).start()
        to_xy(lambda p: ysend.at[g, p], y_rows(g), y_send, y_recv)
        owned = ya.at[z, :, :, pl.ds(pl.multiple_of(g * GROUP, 8), GROUP), :]
        pltpu.make_async_copy(ysend.at[g, pl.ds(2 * z, 2)], owned, own_sem.at[3, g]).start()
        to_z(lambda p: ysend.at[g, pl.ds(2 * p, 2)], owned, v_send.at[0], v_recv.at[0])

    radial(0)
    radial(1)

    @pl.loop(1, ng)
    def _(g):
        radial(g * per)
        span(g - 1)
        radial(g * per + 1)

    span(ng - 1)
    pending.extend([(wb.at[:, pl.ds(0, nz - 1)], w_send), (ysend.at[:, pl.ds(0, nr - 1)], y_send), (ya.at[pl.ds(0, nz - 1)], v_send.at[0])])
    wait(yb.at[:, pl.ds(0, (nr - 1) * bi), :], y_recv)
    for g in range(ng):
        wait(ysend.at[0, 0], own_sem.at[2, g])

    def chol_start(gram):
        ae[:, 0:LANES] = gram
        eye = iota((LANES, LANES), 0) == iota((LANES, LANES), 1)
        ae[:, LANES:] = eye.astype(jnp.float32)

    tiles = range(PIVOTS // 8)
    sub = [iota((8, LANES), 0) + 8 * g for g in tiles]
    lane = iota((PIVOTS, LANES), 1)

    def over_rows(x, t):
        return jnp.broadcast_to(x[t:t + 1, :], (8, LANES))

    def chol_blocks(lo, hi):
        @pl.loop(lo, hi)
        def _(b):
            at = pl.multiple_of(b * PIVOTS, PIVOTS)
            turned = pltpu.roll(ae[pl.ds(at, PIVOTS), 0:LANES], (LANES - b * PIVOTS) % LANES, 1)
            d = [turned[8 * g:8 * g + 8] for g in tiles]
            e = [ae[pl.ds(at + 8 * g, 8), LANES:] for g in tiles]
            cols = [[jnp.broadcast_to(d[g][:, t:t + 1], (8, LANES)) for g in tiles] for t in range(PIVOTS)]
            scale = [jnp.zeros((8, LANES), jnp.float32) for g in tiles]
            for t in range(PIVOTS):
                g0, t0 = t // 8, t % 8
                pivot = over_rows(cols[t][g0], t0)
                r = pltpu.reciprocal(pivot, approx=True)
                r = r * (2.0 - pivot * r)
                f = {g: cols[t][g] * r for g in tiles if g >= g0}
                f[g0] = jnp.where(sub[g0] > t, f[g0], 0.0)
                scale[g0] = jnp.where(sub[g0] == t, lax.rsqrt(pivot), scale[g0])
                for u in range(t + 1, PIVOTS):
                    row = over_rows(cols[u][g0], t0)
                    for g in f:
                        cols[u][g] = cols[u][g] - f[g] * row
                d_row, e_row = over_rows(d[g0], t0), over_rows(e[g0], t0)
                for g in f:
                    d[g] = d[g] - f[g] * d_row
                    e[g] = e[g] - f[g] * e_row
            rows = pltpu.roll(jnp.concatenate([d[g] * scale[g] for g in tiles], axis=0), b * PIVOTS, 1)
            inverse = jnp.concatenate([e[g] * scale[g] for g in tiles], axis=0)
            later = jnp.where(lane >= b * PIVOTS + PIVOTS, rows, 0.0)
            ae[...] -= mm_tn_stacked(later, jnp.concatenate([rows, inverse], axis=1))
            ae[pl.ds(at, PIVOTS), LANES:] = inverse

    def exchange_begin(n):
        to_core(sx.at[n], sr.at[n], x_send.at[n], x_recv.at[n])
        pending.append((sr.at[n], x_send.at[n]))

    def reduce_1(n):
        to_xy(lambda p: part.at[n, pl.ds(pl.multiple_of(p * bi, 8), bi), :], r1.at[n, m], r1_send.at[n], r1_recv.at[n])
        pending.append((r1.at[n, pl.ds(0, nr - 1)], r1_send.at[n]))
        r1[n, m] = part[n, pl.ds(pl.multiple_of(m * bi, 8), bi), :]

    def reduce_2(n):
        wait(r1.at[n, pl.ds(0, nr - 1)], r1_recv.at[n])
        total = r1[n, 0]
        for k in range(1, nr):
            total = total + r1[n, k]
        s1[n] = total
        to_z(lambda p: s1.at[n], r2.at[n, z], r2_send.at[n], r2_recv.at[n])
        pending.append((r2.at[n, pl.ds(0, nz - 1)], r2_send.at[n]))
        r2[n, z] = total

    def reduce_3(n):
        wait(r2.at[n, pl.ds(0, nz - 1)], r2_recv.at[n])
        total = r2[n, 0]
        for k in range(1, nz):
            total = total + r2[n, k]
        s2[n] = total
        mine = pl.ds(pl.multiple_of(m * bi, 8), bi)
        to_xy(lambda p: s2.at[n], im.at[n, mine, :], r3_send.at[n], r3_recv.at[n])
        pending.append((im.at[n, pl.ds(0, (nr - 1) * bi), :], r3_send.at[n]))
        im[n, mine, :] = total

    def reduce_end(n):
        wait(im.at[n, pl.ds(0, (nr - 1) * bi), :], r3_recv.at[n])

    for p in range(2):
        sx[0, p] = mm(f0t[...], yb[p])
    exchange_begin(0)
    wait(sr.at[0], x_recv.at[0])
    part[0] = mm_nt(yb[0], sx[0, 0] + sr[0, 0]) + mm_nt(yb[1], sx[0, 1] + sr[0, 1])
    reduce_1(0)
    yt[0] = yb[0].T
    reduce_2(0)
    wait(ya.at[pl.ds(0, nz - 1)], v_recv.at[0])
    for g in range(ng):
        wait(ysend.at[0, pl.ds(0, 2)], own_sem.at[3, g])
    owned = yo.at[:, pl.ds(pl.multiple_of(m * bi, 8), bi), :]
    pltpu.make_async_copy(ya.at[m // 2, :, m % 2], owned, in_sem.at[3]).start()
    to_xy(lambda p: ya.at[p // 2, :, p % 2], owned, v_send.at[1], v_recv.at[1])
    pending.append((yo.at[:, pl.ds(0, (nr - 1) * bi), :], v_send.at[1]))
    yt[1] = yb[1].T
    reduce_3(0)
    reduce_end(0)

    for p in range(2):
        sx[1, p] = mm(yt[p], im[0])
    exchange_begin(1)
    gx_s[0] = mm(im[0].T, im[0])
    to_core(gx_s.at[0], gr.at[0], g_send.at[0], g_recv.at[0])
    pending.append((gr.at[0], g_send.at[0]))
    wait(sr.at[1], x_recv.at[1])
    part[1] = mm(yb[0], sx[1, 0] + sr[1, 0]) + mm(yb[1], sx[1, 1] + sr[1, 1])
    reduce_1(1)
    blocks = LANES // PIVOTS
    wait(gr.at[0], g_recv.at[0])
    chol_start(gx_s[0] + gr[0])
    chol_blocks(0, 3)
    reduce_2(1)
    wait(yo.at[:, pl.ds(0, (nr - 1) * bi), :], v_recv.at[1])
    wait(ya.at[0, :, 0], in_sem.at[3])
    for q in range(2):
        yot[q] = yo[q].T
    chol_blocks(3, 6)
    reduce_3(1)
    chol_blocks(6, blocks)
    linv[...] = ae[:, LANES:]
    reduce_end(1)
    images = mm_nt(im[1], linv[...])
    gx_s[1] = mm(images.T, images)
    to_core(gx_s.at[1], gr.at[1], g_send.at[1], g_recv.at[1])
    pending.append((gr.at[1], g_send.at[1]))

    for q in range(2):
        sx[2, q] = mm(yot[q], images)
    exchange_begin(2)
    wait(gr.at[1], g_recv.at[1])
    chol_start(gx_s[1] + gr[1])
    chol_blocks(0, blocks)
    wait(sr.at[2], x_recv.at[2])
    for q in range(2):
        out_ref[:, q, :] = mm_nt(ae[:, LANES:], sx[2, q] + sr[2, q])
    finish()


def solution(mesh):
    nr, nz = mesh.shape["rad"], mesh.shape["span"]
    gx = 1
    while gx * gx < nr:
        gx *= 2

    def body(tensor, radial_factor, span_factor, start_factor):
        il = start_factor.shape[0]
        bi = il // nr
        nc, ng = bi // CHUNK, bi // GROUP
        f32 = jnp.float32
        dma = pltpu.SemaphoreType.DMA
        vm = lambda *s: pltpu.VMEM(s, f32)
        scratch = [
            vm(*radial_factor.shape), vm(*span_factor.shape), vm(*start_factor.shape),
            vm(nc, nr, CHUNK * 16, LANES),
            vm(nr, 8, LANES), vm(nz, 8, LANES),
            vm(nz * 8, nr * 16), vm(nr * 16, nz * 64),
            vm(ng, nz, GROUP * 8, LANES), vm(ng, nz, GROUP * 8, LANES),
            vm(ng, nr, 2, GROUP, LANES),
            vm(2, il, LANES), vm(2, LANES, il), vm(LANES, il),
            vm(3, 2, LANES, LANES), vm(3, 2, LANES, LANES),
            vm(2, il, LANES),
            vm(2, nr, bi, LANES), vm(2, bi, LANES),
            vm(2, nz, bi, LANES), vm(2, bi, LANES),
            vm(2, il, LANES),
            vm(2, LANES, LANES), vm(2, LANES, LANES),
            vm(LANES, 2 * LANES), vm(LANES, LANES),
            vm(nz, 2, 2, bi, LANES), vm(2, il, LANES), vm(2, LANES, il),
            dma((4,)), dma((4, nc)),
            dma((2,)), dma((2,)),
            dma, dma((nc,)),
            dma, dma((nc,)),
            dma, dma,
            dma((3,)), dma((3,)),
            dma((2,)), dma((2,)),
            dma((2,)), dma((2,)), dma((2,)), dma((2,)), dma((2,)), dma((2,)),
            dma((2,)), dma((2,)),
        ]
        rows = tensor.reshape(il * 16, LANES)
        hbm = pl.BlockSpec(memory_space=pltpu.HBM)
        core = pl.pallas_call(
            functools.partial(kernel, nr, nz, gx),
            out_shape=jax.ShapeDtypeStruct((LANES, 2, LANES), f32),
            in_specs=[hbm] * 4,
            out_specs=pl.BlockSpec(memory_space=pltpu.VMEM),
            scratch_shapes=scratch,
            compiler_params=pltpu.CompilerParams(collective_id=0, has_side_effects=True, vmem_limit_bytes=62 * 1024 * 1024),
        )(rows, radial_factor, span_factor, start_factor)
        return core.reshape(LANES, 1, 2, LANES)

    in_specs = (P("ax", "rad", "span", None), P("rad", None), P("span", None), P("ax", None))
    out_specs = P(None, "rad", "span", None)
    return jax.shard_map(body, mesh=mesh, in_specs=in_specs, out_specs=out_specs, check_vma=False)
```

```python
import functools

import jax
import jax.numpy as jnp
from jax import lax
from jax.experimental import pallas as pl
from jax.experimental.pallas import tpu as pltpu
from jax.sharding import PartitionSpec as P

MESH = pl.DeviceIdType.MESH
HIGHEST = lax.Precision.HIGHEST
LANES = 128
CHUNK = 4
GROUP = 8
PIVOTS = 16


def mm(a, b):
    return lax.dot_general(a, b, (((1,), (0,)), ((), ())), precision=HIGHEST, preferred_element_type=jnp.float32)


def mm_nt(a, b):
    return lax.dot_general(a, b, (((1,), (1,)), ((), ())), precision=HIGHEST, preferred_element_type=jnp.float32)


def mm_tn(a, b):
    return lax.dot_general(a, b, (((0,), (0,)), ((), ())), precision=HIGHEST, preferred_element_type=jnp.float32)


def split3(x):
    high = x.astype(jnp.bfloat16)
    rest = x - high.astype(jnp.float32)
    mid = rest.astype(jnp.bfloat16)
    return high, mid, (rest - mid.astype(jnp.float32)).astype(jnp.bfloat16)


def mm_tn_stacked(a, b):
    ah, am, al = split3(a)
    bh, bm, bl = split3(b)
    left = jnp.concatenate([ah, ah, ah, am, am, al], axis=0)
    right = jnp.concatenate([bh, bm, bl, bh, bm, bh], axis=0)
    return lax.dot_general(left, right, (((0,), (0,)), ((), ())), preferred_element_type=jnp.float32)


def iota(shape, dim):
    return lax.broadcasted_iota(jnp.int32, shape, dim)


def kernel(nr, nz, gx, t_ref, a_ref, b_ref, f_ref, out_ref,
           av, bv, fv, xb, ag, bg, ma, mb, ub, wb, ysend, yb, yt, f0t,
           sx, sr, part, r1, s1, r2, s2, im, gx_s, gr, ae, linv, ya, yo, yot,
           in_sem, own_sem, ab_send, ab_recv, t_send, t_recv, w_send, w_recv, y_send, y_recv,
           x_send, x_recv, g_send, g_recv, r1_send, r1_recv, r2_send, r2_recv, r3_send, r3_recv,
           v_send, v_recv):
    c = lax.axis_index("ax")
    m = lax.axis_index("rad")
    z = lax.axis_index("span")
    gy = nr // gx
    rj, rk = 2 * nz, nr
    il = f_ref.shape[0]
    bi = il // nr
    nc, ng, per = bi // CHUNK, bi // GROUP, GROUP // CHUNK
    my, mx = m // gx, m % gx

    xs = [lax.rem(mx + d, gx) for d in range(gx)]
    ys = [lax.rem(my + d, gy) * gx for d in range(gy)]
    steps = [(dy, dx) for dy in range(gy) for dx in range(gx) if dy or dx]
    near_first = [ys[dy] + xs[dx] for dy, dx in steps]
    steps.sort(key=lambda s: -min(s[0], gy - s[0]) - min(s[1], gx - s[1]))
    xy_peers = [ys[dy] + xs[dx] for dy, dx in steps]
    z_peers = [lax.rem(z + d, nz) for d in sorted(range(1, nz), key=lambda d: -min(d, nz - d))]

    def remote(src, dst, send, recv, dev):
        return pltpu.make_async_remote_copy(src_ref=src, dst_ref=dst, send_sem=send, recv_sem=recv, device_id=dev, device_id_type=MESH)

    def to_xy(src_of, dst, send, recv, peers=xy_peers):
        for peer in peers:
            remote(src_of(peer), dst, send, recv, (c, peer, z)).start()

    def to_z(src_of, dst, send, recv):
        for peer in z_peers:
            remote(src_of(peer), dst, send, recv, (c, m, peer)).start()

    def to_core(src, dst, send, recv):
        remote(src, dst, send, recv, (1 - c, m, z)).start()

    def wait(view, sem):
        pltpu.make_async_copy(view, view, sem).wait()

    pending = []

    def finish():
        for view, sem in pending:
            wait(view, sem)

    arriving = [pltpu.make_async_copy(src, dst, in_sem.at[n]) for n, (src, dst) in enumerate(((a_ref, av), (b_ref, bv), (f_ref, fv)))]
    for copy in arriving:
        copy.start()

    barrier = pltpu.get_barrier_semaphore()

    def greet(dev):
        pl.semaphore_signal(barrier, inc=1, device_id=dev, device_id_type=MESH)

    for peer in xy_peers:
        greet((c, peer, z))
    for peer in z_peers:
        greet((c, m, peer))
    greet((1 - c, m, z))
    arriving[0].wait()
    arriving[1].wait()
    ag[m] = jnp.zeros((8, LANES), jnp.float32)
    ag[m, 0:4, 0:rj] = av[...]
    bg[z] = jnp.zeros((8, LANES), jnp.float32)
    bg[z, 0:4, 0:rk] = bv[...]
    pl.semaphore_wait(barrier, (nr - 1) + (nz - 1) + 1)

    to_xy(lambda p: ag.at[m], ag.at[m], ab_send.at[0], ab_recv.at[0])
    pending.append((ag.at[pl.ds(0, nr - 1)], ab_send.at[0]))
    to_z(lambda p: bg.at[z], bg.at[z], ab_send.at[1], ab_recv.at[1])
    pending.append((bg.at[pl.ds(0, nz - 1)], ab_send.at[1]))

    def t_rows(peer, k):
        return t_ref.at[pl.ds(pl.multiple_of((peer * bi + k * CHUNK) * 16, 64), CHUNK * 16), :]

    @pl.loop(0, nc)
    def _(k):
        pltpu.make_async_copy(t_rows(m, k), xb.at[k, m], own_sem.at[0, k]).start()
        to_xy(lambda p: t_rows(p, k), xb.at[k, m], t_send, t_recv.at[k], near_first)

    pending.append((xb.at[:, pl.ds(0, nr - 1)], t_send))
    arriving[2].wait()
    f0t[...] = fv[...].T

    wait(ag.at[pl.ds(0, nr - 1)], ab_recv.at[0])
    wait(bg.at[pl.ds(0, nz - 1)], ab_recv.at[1])

    rows, cols = rj * 4, nr * 16
    pick = (iota((rows, LANES), 0) // 4 == iota((rows, LANES), 1)).astype(jnp.float32)
    spread_row, spread_col = iota((nr * 8, cols), 0), iota((nr * 8, cols), 1)
    spread = (spread_row == (spread_col // 16) * 8 + (spread_col % 16) // 4).astype(jnp.float32)
    full = mm(mm_nt(pick, ag[...].reshape(nr * 8, LANES)), spread)
    ma[...] = jnp.where(iota((rows, cols), 0) % 4 == iota((rows, cols), 1) % 4, full, 0.0)

    rows, cols = rk * 16, nz * 64
    pick = (iota((rows, LANES), 0) // 16 == iota((rows, LANES), 1)).astype(jnp.float32)
    spread_row, spread_col = iota((nz * 8, cols), 0), iota((nz * 8, cols), 1)
    spread = (spread_row == (spread_col // 64) * 8 + spread_col % 4).astype(jnp.float32)
    full = mm(mm_nt(pick, bg[...].reshape(nz * 8, LANES)), spread)
    row, col = iota((rows, cols), 0), iota((rows, cols), 1)
    same = jnp.logical_and((row // 8) % 2 == (col // 4) % 2, row % 8 == (col // 8) % 8)
    mb[...] = jnp.where(same, full, 0.0)

    def radial(k):
        wait(xb.at[k, pl.ds(0, nr - 1)], t_recv.at[k])
        wait(xb.at[k, 0], own_sem.at[0, k])

        @pl.loop(0, CHUNK // 2)
        def _(h):
            at = pl.multiple_of(h * 32, 32)
            both = xb[k, :, pl.ds(at, 32), :]
            x0 = both[:, 0:16, :].reshape(nr * 16, LANES)
            x1 = both[:, 16:32, :].reshape(nr * 16, LANES)
            u = mm(ma[...], jnp.concatenate([x0, x1], axis=1))
            at8 = pl.multiple_of((k % per) * CHUNK * 8 + h * 16, 16)
            ub[k // per, :, pl.ds(at8, 8), :] = u[:, 0:LANES].reshape(nz, 8, LANES)
            ub[k // per, :, pl.ds(at8 + 8, 8), :] = u[:, LANES:].reshape(nz, 8, LANES)

        g, half = k // per, pl.ds(pl.multiple_of((k % per) * CHUNK * 8, CHUNK * 8), CHUNK * 8)
        pltpu.make_async_copy(ub.at[g, z, half], wb.at[g, z, half], own_sem.at[1, k]).start()
        to_z(lambda p: ub.at[g, p, half], wb.at[g, z, half], w_send, w_recv.at[k])

    def y_rows(g):
        return yb.at[:, pl.ds(pl.multiple_of(m * bi + g * GROUP, 8), GROUP), :]

    def span(g):
        for h in range(per):
            wait(wb.at[g, pl.ds(0, nz - 1), pl.ds(0, CHUNK * 8)], w_recv.at[g * per + h])
            wait(wb.at[g, 0, pl.ds(0, CHUNK * 8)], own_sem.at[1, g * per + h])
        y = mm(mb[...], wb[g].reshape(nz * 64, LANES))
        ysend[g] = y.reshape(nr, 2, GROUP, LANES)
        pltpu.make_async_copy(ysend.at[g, m], y_rows(g), own_sem.at[2, g]).start()
        to_xy(lambda p: ysend.at[g, p], y_rows(g), y_send, y_recv)
        owned = ya.at[z, :, :, pl.ds(pl.multiple_of(g * GROUP, 8), GROUP), :]
        pltpu.make_async_copy(ysend.at[g, pl.ds(2 * z, 2)], owned, own_sem.at[3, g]).start()
        to_z(lambda p: ysend.at[g, pl.ds(2 * p, 2)], owned, v_send.at[0], v_recv.at[0])

    radial(0)
    radial(1)

    @pl.loop(1, ng)
    def _(g):
        radial(g * per)
        span(g - 1)
        radial(g * per + 1)

    span(ng - 1)
    pending.extend([(wb.at[:, pl.ds(0, nz - 1)], w_send), (ysend.at[:, pl.ds(0, nr - 1)], y_send), (ya.at[pl.ds(0, nz - 1)], v_send.at[0])])
    wait(yb.at[:, pl.ds(0, (nr - 1) * bi), :], y_recv)
    for g in range(ng):
        wait(ysend.at[0, 0], own_sem.at[2, g])

    def chol_start(gram):
        ae[:, 0:LANES] = gram
        eye = iota((LANES, LANES), 0) == iota((LANES, LANES), 1)
        ae[:, LANES:] = eye.astype(jnp.float32)

    tiles = range(PIVOTS // 8)
    sub = [iota((8, LANES), 0) + 8 * g for g in tiles]
    lane = iota((PIVOTS, LANES), 1)

    def over_rows(x, t):
        return jnp.broadcast_to(x[t:t + 1, :], (8, LANES))

    def chol_blocks(lo, hi):
        @pl.loop(lo, hi)
        def _(b):
            at = pl.multiple_of(b * PIVOTS, PIVOTS)
            turned = pltpu.roll(ae[pl.ds(at, PIVOTS), 0:LANES], (LANES - b * PIVOTS) % LANES, 1)
            d = [turned[8 * g:8 * g + 8] for g in tiles]
            e = [ae[pl.ds(at + 8 * g, 8), LANES:] for g in tiles]
            cols = [[jnp.broadcast_to(d[g][:, t:t + 1], (8, LANES)) for g in tiles] for t in range(PIVOTS)]
            scale = [jnp.zeros((8, LANES), jnp.float32) for g in tiles]
            for t in range(PIVOTS):
                g0, t0 = t // 8, t % 8
                pivot = over_rows(cols[t][g0], t0)
                r = pltpu.reciprocal(pivot, approx=True)
                r = r * (2.0 - pivot * r)
                f = {g: cols[t][g] * r for g in tiles if g >= g0}
                f[g0] = jnp.where(sub[g0] > t, f[g0], 0.0)
                scale[g0] = jnp.where(sub[g0] == t, lax.rsqrt(pivot), scale[g0])
                for u in range(t + 1, PIVOTS):
                    row = over_rows(cols[u][g0], t0)
                    for g in f:
                        cols[u][g] = cols[u][g] - f[g] * row
                d_row, e_row = over_rows(d[g0], t0), over_rows(e[g0], t0)
                for g in f:
                    d[g] = d[g] - f[g] * d_row
                    e[g] = e[g] - f[g] * e_row
            rows = pltpu.roll(jnp.concatenate([d[g] * scale[g] for g in tiles], axis=0), b * PIVOTS, 1)
            inverse = jnp.concatenate([e[g] * scale[g] for g in tiles], axis=0)
            later = jnp.where(lane >= b * PIVOTS + PIVOTS, rows, 0.0)
            ae[...] -= mm_tn_stacked(later, jnp.concatenate([rows, inverse], axis=1))
            ae[pl.ds(at, PIVOTS), LANES:] = inverse

    def exchange_begin(n):
        to_core(sx.at[n], sr.at[n], x_send.at[n], x_recv.at[n])
        pending.append((sr.at[n], x_send.at[n]))

    def reduce_1(n):
        to_xy(lambda p: part.at[n, pl.ds(pl.multiple_of(p * bi, 8), bi), :], r1.at[n, m], r1_send.at[n], r1_recv.at[n])
        pending.append((r1.at[n, pl.ds(0, nr - 1)], r1_send.at[n]))
        r1[n, m] = part[n, pl.ds(pl.multiple_of(m * bi, 8), bi), :]

    def reduce_2(n):
        wait(r1.at[n, pl.ds(0, nr - 1)], r1_recv.at[n])
        total = r1[n, 0]
        for k in range(1, nr):
            total = total + r1[n, k]
        s1[n] = total
        to_z(lambda p: s1.at[n], r2.at[n, z], r2_send.at[n], r2_recv.at[n])
        pending.append((r2.at[n, pl.ds(0, nz - 1)], r2_send.at[n]))
        r2[n, z] = total

    def reduce_3(n):
        wait(r2.at[n, pl.ds(0, nz - 1)], r2_recv.at[n])
        total = r2[n, 0]
        for k in range(1, nz):
            total = total + r2[n, k]
        s2[n] = total
        mine = pl.ds(pl.multiple_of(m * bi, 8), bi)
        to_xy(lambda p: s2.at[n], im.at[n, mine, :], r3_send.at[n], r3_recv.at[n])
        pending.append((im.at[n, pl.ds(0, (nr - 1) * bi), :], r3_send.at[n]))
        im[n, mine, :] = total

    def reduce_end(n):
        wait(im.at[n, pl.ds(0, (nr - 1) * bi), :], r3_recv.at[n])

    def unfolded():
        return jnp.concatenate([yb[0], yb[1]], axis=1)

    both = mm(f0t[...], unfolded())
    for p in range(2):
        sx[0, p] = both[:, p * LANES:(p + 1) * LANES]
    exchange_begin(0)
    wait(sr.at[0], x_recv.at[0])
    part[0] = mm_nt(unfolded(), jnp.concatenate([sx[0, p] + sr[0, p] for p in range(2)], axis=1))
    reduce_1(0)
    yt[0] = yb[0].T
    reduce_2(0)
    wait(ya.at[pl.ds(0, nz - 1)], v_recv.at[0])
    for g in range(ng):
        wait(ysend.at[0, pl.ds(0, 2)], own_sem.at[3, g])
    owned = yo.at[:, pl.ds(pl.multiple_of(m * bi, 8), bi), :]
    pltpu.make_async_copy(ya.at[m // 2, :, m % 2], owned, in_sem.at[3]).start()
    to_xy(lambda p: ya.at[p // 2, :, p % 2], owned, v_send.at[1], v_recv.at[1])
    pending.append((yo.at[:, pl.ds(0, (nr - 1) * bi), :], v_send.at[1]))
    yt[1] = yb[1].T
    reduce_3(0)
    reduce_end(0)

    sx[1] = mm(yt[...].reshape(2 * LANES, il), im[0]).reshape(2, LANES, LANES)
    exchange_begin(1)
    gx_s[0] = mm_tn(im[0], im[0])
    to_core(gx_s.at[0], gr.at[0], g_send.at[0], g_recv.at[0])
    pending.append((gr.at[0], g_send.at[0]))
    wait(sr.at[1], x_recv.at[1])
    part[1] = mm(unfolded(), (sx[1] + sr[1]).reshape(2 * LANES, LANES))
    reduce_1(1)
    blocks = LANES // PIVOTS
    wait(gr.at[0], g_recv.at[0])
    chol_start(gx_s[0] + gr[0])
    chol_blocks(0, 3)
    reduce_2(1)
    wait(yo.at[:, pl.ds(0, (nr - 1) * bi), :], v_recv.at[1])
    wait(ya.at[0, :, 0], in_sem.at[3])
    for q in range(2):
        yot[q] = yo[q].T
    chol_blocks(3, 6)
    reduce_3(1)
    chol_blocks(6, blocks)
    linv[...] = ae[:, LANES:]
    reduce_end(1)
    images = mm_nt(im[1], linv[...])
    gx_s[1] = mm_tn(images, images)
    to_core(gx_s.at[1], gr.at[1], g_send.at[1], g_recv.at[1])
    pending.append((gr.at[1], g_send.at[1]))

    sx[2] = mm(yot[...].reshape(2 * LANES, il), images).reshape(2, LANES, LANES)
    exchange_begin(2)
    wait(gr.at[1], g_recv.at[1])
    chol_start(gx_s[1] + gr[1])
    chol_blocks(0, blocks)
    wait(sr.at[2], x_recv.at[2])
    for q in range(2):
        out_ref[:, q, :] = mm_nt(ae[:, LANES:], sx[2, q] + sr[2, q])
    finish()


def solution(mesh):
    nr, nz = mesh.shape["rad"], mesh.shape["span"]
    gx = 1
    while gx * gx < nr:
        gx *= 2

    def body(tensor, radial_factor, span_factor, start_factor):
        il = start_factor.shape[0]
        bi = il // nr
        nc, ng = bi // CHUNK, bi // GROUP
        f32 = jnp.float32
        dma = pltpu.SemaphoreType.DMA
        vm = lambda *s: pltpu.VMEM(s, f32)
        scratch = [
            vm(*radial_factor.shape), vm(*span_factor.shape), vm(*start_factor.shape),
            vm(nc, nr, CHUNK * 16, LANES),
            vm(nr, 8, LANES), vm(nz, 8, LANES),
            vm(nz * 8, nr * 16), vm(nr * 16, nz * 64),
            vm(ng, nz, GROUP * 8, LANES), vm(ng, nz, GROUP * 8, LANES),
            vm(ng, nr, 2, GROUP, LANES),
            vm(2, il, LANES), vm(2, LANES, il), vm(LANES, il),
            vm(3, 2, LANES, LANES), vm(3, 2, LANES, LANES),
            vm(2, il, LANES),
            vm(2, nr, bi, LANES), vm(2, bi, LANES),
            vm(2, nz, bi, LANES), vm(2, bi, LANES),
            vm(2, il, LANES),
            vm(2, LANES, LANES), vm(2, LANES, LANES),
            vm(LANES, 2 * LANES), vm(LANES, LANES),
            vm(nz, 2, 2, bi, LANES), vm(2, il, LANES), vm(2, LANES, il),
            dma((4,)), dma((4, nc)),
            dma((2,)), dma((2,)),
            dma, dma((nc,)),
            dma, dma((nc,)),
            dma, dma,
            dma((3,)), dma((3,)),
            dma((2,)), dma((2,)),
            dma((2,)), dma((2,)), dma((2,)), dma((2,)), dma((2,)), dma((2,)),
            dma((2,)), dma((2,)),
        ]
        rows = tensor.reshape(il * 16, LANES)
        hbm = pl.BlockSpec(memory_space=pltpu.HBM)
        core = pl.pallas_call(
            functools.partial(kernel, nr, nz, gx),
            out_shape=jax.ShapeDtypeStruct((LANES, 2, LANES), f32),
            in_specs=[hbm] * 4,
            out_specs=pl.BlockSpec(memory_space=pltpu.VMEM),
            scratch_shapes=scratch,
            compiler_params=pltpu.CompilerParams(collective_id=0, has_side_effects=True, vmem_limit_bytes=62 * 1024 * 1024),
        )(rows, radial_factor, span_factor, start_factor)
        return core.reshape(LANES, 1, 2, LANES)

    in_specs = (P("ax", "rad", "span", None), P("rad", None), P("span", None), P("ax", None))
    out_specs = P(None, "rad", "span", None)
    return jax.shard_map(body, mesh=mesh, in_specs=in_specs, out_specs=out_specs, check_vma=False)
```

```python
import functools

import jax
import jax.numpy as jnp
from jax import lax
from jax.experimental import pallas as pl
from jax.experimental.pallas import tpu as pltpu
from jax.sharding import PartitionSpec as P

MESH = pl.DeviceIdType.MESH
HIGHEST = lax.Precision.HIGHEST
LANES = 128
CHUNK = 4
GROUP = 8
PIVOTS = 16


def mm(a, b):
    return lax.dot_general(a, b, (((1,), (0,)), ((), ())), precision=HIGHEST, preferred_element_type=jnp.float32)


def mm_nt(a, b):
    return lax.dot_general(a, b, (((1,), (1,)), ((), ())), precision=HIGHEST, preferred_element_type=jnp.float32)


def mm_tn(a, b):
    return lax.dot_general(a, b, (((0,), (0,)), ((), ())), precision=HIGHEST, preferred_element_type=jnp.float32)


def split3(x):
    high = x.astype(jnp.bfloat16)
    rest = x - high.astype(jnp.float32)
    mid = rest.astype(jnp.bfloat16)
    return high, mid, (rest - mid.astype(jnp.float32)).astype(jnp.bfloat16)


def mm_tn_stacked(a, b):
    ah, am, al = split3(a)
    bh, bm, bl = split3(b)
    left = jnp.concatenate([ah, ah, ah, am, am, al], axis=0)
    right = jnp.concatenate([bh, bm, bl, bh, bm, bh], axis=0)
    return lax.dot_general(left, right, (((0,), (0,)), ((), ())), preferred_element_type=jnp.float32)


def iota(shape, dim):
    return lax.broadcasted_iota(jnp.int32, shape, dim)


def kernel(nr, nz, gx, t_ref, a_ref, b_ref, f_ref, out_ref,
           av, bv, fv, xb, ag, bg, ma, mb, ub, wb, ysend, yb, yt, f0t,
           sx, sr, part, r1, s1, r2, s2, im, gx_s, gr, ae, linv, ya, yo, yd,
           xz, zm, rm, vs, vr, yz,
           in_sem, own_sem, ab_send, ab_recv, t_send, t_recv, w_send, w_recv, y_send, y_recv,
           x_send, x_recv, g_send, g_recv, r1_send, r1_recv, r2_send, r2_recv, r3_send, r3_recv,
           v_send, v_recv, q_send, q_recv, u_recv):
    c = lax.axis_index("ax")
    m = lax.axis_index("rad")
    z = lax.axis_index("span")
    gy = nr // gx
    rj, rk = 2 * nz, nr
    il = f_ref.shape[0]
    bi = il // nr
    pb = bi - bi // 4
    zb = (il - nr * pb) // nz
    nc, ng, per, nq = pb // CHUNK, pb // GROUP, GROUP // CHUNK, zb // CHUNK
    my, mx = m // gx, m % gx

    xs = [lax.rem(mx + d, gx) for d in range(gx)]
    ys = [lax.rem(my + d, gy) * gx for d in range(gy)]
    steps = [(dy, dx) for dy in range(gy) for dx in range(gx) if dy or dx]
    near_first = [ys[dy] + xs[dx] for dy, dx in steps]
    steps.sort(key=lambda s: -min(s[0], gy - s[0]) - min(s[1], gx - s[1]))
    xy_peers = [ys[dy] + xs[dx] for dy, dx in steps]
    z_peers = [lax.rem(z + d, nz) for d in sorted(range(1, nz), key=lambda d: -min(d, nz - d))]

    def remote(src, dst, send, recv, dev):
        return pltpu.make_async_remote_copy(src_ref=src, dst_ref=dst, send_sem=send, recv_sem=recv, device_id=dev, device_id_type=MESH)

    def to_xy(src_of, dst, send, recv, peers=xy_peers):
        for peer in peers:
            remote(src_of(peer), dst, send, recv, (c, peer, z)).start()

    def to_z(src_of, dst, send, recv):
        for peer in z_peers:
            remote(src_of(peer), dst, send, recv, (c, m, peer)).start()

    def to_core(src, dst, send, recv):
        remote(src, dst, send, recv, (1 - c, m, z)).start()

    def wait(view, sem):
        pltpu.make_async_copy(view, view, sem).wait()

    pending = []

    def finish():
        for view, sem in pending:
            wait(view, sem)

    arriving = [pltpu.make_async_copy(src, dst, in_sem.at[n]) for n, (src, dst) in enumerate(((a_ref, av), (b_ref, bv), (f_ref, fv)))]
    for copy in arriving:
        copy.start()

    barrier = pltpu.get_barrier_semaphore()

    def greet(dev):
        pl.semaphore_signal(barrier, inc=1, device_id=dev, device_id_type=MESH)

    for peer in xy_peers:
        greet((c, peer, z))
    for peer in z_peers:
        greet((c, m, peer))
    greet((1 - c, m, z))
    arriving[0].wait()
    arriving[1].wait()
    ag[m] = jnp.zeros((8, LANES), jnp.float32)
    ag[m, 0:4, 0:rj] = av[...]
    bg[z] = jnp.zeros((8, LANES), jnp.float32)
    bg[z, 0:4, 0:rk] = bv[...]
    pl.semaphore_wait(barrier, (nr - 1) + (nz - 1) + 1)

    to_xy(lambda p: ag.at[m], ag.at[m], ab_send.at[0], ab_recv.at[0])
    pending.append((ag.at[pl.ds(0, nr - 1)], ab_send.at[0]))
    to_z(lambda p: bg.at[z], bg.at[z], ab_send.at[1], ab_recv.at[1])
    pending.append((bg.at[pl.ds(0, nz - 1)], ab_send.at[1]))

    def t_rows(peer, k):
        return t_ref.at[pl.ds(pl.multiple_of((peer * pb + k * CHUNK) * 16, 64), CHUNK * 16), :]

    def t_ring(peer, k):
        return t_ref.at[pl.ds(pl.multiple_of((nr * pb + peer * zb + k * CHUNK) * 16, 64), CHUNK * 16), :]

    def to_plane(k):
        pltpu.make_async_copy(t_rows(m, k), xb.at[k, m], own_sem.at[0, k]).start()
        to_xy(lambda p: t_rows(p, k), xb.at[k, m], t_send, t_recv.at[k], near_first)

    @pl.loop(0, nq)
    def _(k):
        pltpu.make_async_copy(t_ring(z, k), xz.at[k, z], own_sem.at[4, k]).start()
        to_z(lambda p: t_ring(p, k), xz.at[k, z], q_send.at[0], q_recv.at[k])
        to_plane(k)

    @pl.loop(nq, nc)
    def _(k):
        to_plane(k)

    pending.append((xb.at[:, pl.ds(0, nr - 1)], t_send))
    pending.append((xz.at[:, pl.ds(0, nz - 1)], q_send.at[0]))
    arriving[2].wait()
    f0t[...] = fv[...].T

    wait(ag.at[pl.ds(0, nr - 1)], ab_recv.at[0])
    wait(bg.at[pl.ds(0, nz - 1)], ab_recv.at[1])

    def spread(gathered, shape, row_div, col_div, col_of, same):
        rows, cols = shape
        n = gathered.shape[0] * 8
        pick = (iota((rows, LANES), 0) // row_div == iota((rows, LANES), 1)).astype(jnp.float32)
        at, col = iota((n, cols), 0), iota((n, cols), 1)
        place = (at == (col // col_div) * 8 + col_of(col)).astype(jnp.float32)
        full = mm(mm_nt(pick, gathered[...].reshape(n, LANES)), place)
        return jnp.where(same(iota(shape, 0), iota(shape, 1)), full, 0.0)

    ma[...] = spread(ag, ma.shape, 4, 16, lambda col: (col % 16) // 4, lambda r, col: r % 4 == col % 4)
    mb[...] = spread(bg, mb.shape, 16, 64, lambda col: col % 4, lambda r, col: jnp.logical_and(
        (r // 8) % 2 == (col // 4) % 2, r % 8 == (col // 8) % 8))
    zm[...] = spread(bg, zm.shape, 8, 32, lambda col: col % 4, lambda r, col: r % 8 == (col // 4) % 8)
    rm[...] = spread(ag, rm.shape, 8, 32, lambda col: col % 4, lambda r, col: r % 8 == (col // 4) % 8)

    def radial(k):
        wait(xb.at[k, pl.ds(0, nr - 1)], t_recv.at[k])
        wait(xb.at[k, 0], own_sem.at[0, k])

        @pl.loop(0, CHUNK // 2)
        def _(h):
            at = pl.multiple_of(h * 32, 32)
            both = xb[k, :, pl.ds(at, 32), :]
            x0 = both[:, 0:16, :].reshape(nr * 16, LANES)
            x1 = both[:, 16:32, :].reshape(nr * 16, LANES)
            u = mm(ma[...], jnp.concatenate([x0, x1], axis=1))
            at8 = pl.multiple_of((k % per) * CHUNK * 8 + h * 16, 16)
            ub[k // per, :, pl.ds(at8, 8), :] = u[:, 0:LANES].reshape(nz, 8, LANES)
            ub[k // per, :, pl.ds(at8 + 8, 8), :] = u[:, LANES:].reshape(nz, 8, LANES)

        g, half = k // per, pl.ds(pl.multiple_of((k % per) * CHUNK * 8, CHUNK * 8), CHUNK * 8)
        pltpu.make_async_copy(ub.at[g, z, half], wb.at[g, z, half], own_sem.at[1, k]).start()
        to_z(lambda p: ub.at[g, p, half], wb.at[g, z, half], w_send, w_recv.at[k])

    def y_rows(g):
        return yb.at[:, pl.ds(pl.multiple_of(m * pb + g * GROUP, 8), GROUP), :]

    def span(g):
        for h in range(per):
            wait(wb.at[g, pl.ds(0, nz - 1), pl.ds(0, CHUNK * 8)], w_recv.at[g * per + h])
            wait(wb.at[g, 0, pl.ds(0, CHUNK * 8)], own_sem.at[1, g * per + h])
        y = mm(mb[...], wb[g].reshape(nz * 64, LANES))
        ysend[g] = y.reshape(nr, 2, GROUP, LANES)
        pltpu.make_async_copy(ysend.at[g, m], y_rows(g), own_sem.at[2, g]).start()
        to_xy(lambda p: ysend.at[g, p], y_rows(g), y_send, y_recv)

    def ring_span(k):
        wait(xz.at[k, pl.ds(0, nz - 1)], q_recv.at[k])
        wait(xz.at[k, 0], own_sem.at[4, k])
        for h in range(CHUNK // 2):
            rows = xz[k, :, pl.ds(h * 32, 32), :].reshape(nz * 32, LANES)
            vs[:, pl.ds((k * 2 + h) * 8, 8), :] = mm(zm[...], rows).reshape(nr, 8, LANES)
        if k % per == per - 1:
            rows = pl.ds((k // per) * GROUP * 4, GROUP * 4)
            pltpu.make_async_copy(vs.at[m, rows], vr.at[m, rows], own_sem.at[5, k // per]).start()
            to_xy(lambda p: vs.at[p, rows], vr.at[m, rows], q_send.at[1], u_recv.at[k // per])

    def ring_y(g):
        return yb.at[:, pl.ds(pl.multiple_of(nr * pb + z * zb + g * GROUP, 8), GROUP), :]

    def ring_radial(g):
        rows, part_rows = pl.ds(g * GROUP * 4, GROUP * 4), pl.ds(g * GROUP, GROUP)
        wait(vr.at[pl.ds(0, nr - 1), rows], u_recv.at[g])
        wait(vr.at[0, rows], own_sem.at[5, g])
        y = mm(rm[...], vr[:, rows, :].reshape(nr * 32, LANES))
        yz[:, part_rows, :] = y.reshape(rj, GROUP, LANES)
        pltpu.make_async_copy(yz.at[pl.ds(2 * z, 2), part_rows], ring_y(g), own_sem.at[6, g]).start()
        to_z(lambda p: yz.at[pl.ds(2 * p, 2), part_rows], ring_y(g), q_send.at[2], q_recv.at[nq])

    radial(0)
    radial(1)
    ring_span(0)
    radial(2)
    span(0)
    ring_span(1)
    radial(3)
    ring_span(2)
    radial(4)
    span(1)
    ring_span(3)
    radial(5)
    ring_radial(0)
    span(2)
    ring_radial(1)
    pending.extend([(wb.at[:, pl.ds(0, nz - 1)], w_send), (ysend.at[:, pl.ds(0, nr - 1)], y_send)])
    pending.extend([(vr.at[pl.ds(0, nr - 1)], q_send.at[1]), (yb.at[:, pl.ds(0, (nz - 1) * zb), :], q_send.at[2])])
    wait(yb.at[:, pl.ds(0, (nr - 1) * pb), :], y_recv)
    wait(yb.at[:, pl.ds(0, (nz - 1) * zb), :], q_recv.at[nq])
    for g in range(ng):
        wait(ysend.at[0, 0], own_sem.at[2, g])
    for g in range(zb // GROUP):
        wait(yz.at[pl.ds(0, 2), pl.ds(0, GROUP)], own_sem.at[6, g])

    def owned_z(g):
        owned = ya.at[z, :, :, pl.ds(g * GROUP, GROUP), :]
        pltpu.make_async_copy(ysend.at[g, pl.ds(2 * z, 2)], owned, own_sem.at[3, g]).start()
        to_z(lambda p: ysend.at[g, pl.ds(2 * p, 2)], owned, v_send.at[0], v_recv.at[0])

    def owned_xy():
        pending.append((ya.at[pl.ds(0, nz - 1)], v_send.at[0]))
        wait(ya.at[pl.ds(0, nz - 1)], v_recv.at[0])
        for g in range(ng):
            wait(ysend.at[0, pl.ds(0, 2)], own_sem.at[3, g])
        owned = yo.at[:, pl.ds(pl.multiple_of(m * pb, 8), pb), :]
        pltpu.make_async_copy(ya.at[m // 2, :, m % 2], owned, in_sem.at[3]).start()
        to_xy(lambda p: ya.at[p // 2, :, p % 2], owned, v_send.at[1], v_recv.at[1])
        pending.append((yo.at[:, pl.ds(0, (nr - 1) * pb), :], v_send.at[1]))

    def ring_owned_xy():
        pltpu.make_async_copy(yz.at[m], yd.at[m], in_sem.at[4]).start()
        to_xy(lambda p: yz.at[p], yd.at[m], v_send.at[2], v_recv.at[2])
        pending.append((yd.at[pl.ds(0, nr - 1)], v_send.at[2]))

    def ring_owned_z():
        wait(yd.at[pl.ds(0, nr - 1)], v_recv.at[2])
        wait(yd.at[0], in_sem.at[4])
        owned = yo.at[:, pl.ds(pl.multiple_of(nr * pb + z * zb, 8), zb), :]
        pltpu.make_async_copy(yd.at[pl.ds(2 * z, 2)], owned, in_sem.at[5]).start()
        to_z(lambda p: yd.at[pl.ds(2 * p, 2)], owned, v_send.at[3], v_recv.at[3])
        pending.append((yo.at[:, pl.ds(0, (nz - 1) * zb), :], v_send.at[3]))

    def owned_end():
        wait(yo.at[:, pl.ds(0, (nr - 1) * pb), :], v_recv.at[1])
        wait(ya.at[0, :, 0], in_sem.at[3])
        wait(yo.at[:, pl.ds(0, (nz - 1) * zb), :], v_recv.at[3])
        wait(yd.at[pl.ds(0, 2)], in_sem.at[5])

    def chol_start(gram):
        ae[:, 0:LANES] = gram
        eye = iota((LANES, LANES), 0) == iota((LANES, LANES), 1)
        ae[:, LANES:] = eye.astype(jnp.float32)

    tiles = range(PIVOTS // 8)
    sub = [iota((8, LANES), 0) + 8 * g for g in tiles]
    lane = iota((PIVOTS, LANES), 1)

    def over_rows(x, t):
        return jnp.broadcast_to(x[t:t + 1, :], (8, LANES))

    def chol_blocks(lo, hi):
        @pl.loop(lo, hi)
        def _(b):
            at = pl.multiple_of(b * PIVOTS, PIVOTS)
            turned = pltpu.roll(ae[pl.ds(at, PIVOTS), 0:LANES], (LANES - b * PIVOTS) % LANES, 1)
            d = [turned[8 * g:8 * g + 8] for g in tiles]
            e = [ae[pl.ds(at + 8 * g, 8), LANES:] for g in tiles]
            cols = [[jnp.broadcast_to(d[g][:, t:t + 1], (8, LANES)) for g in tiles] for t in range(PIVOTS)]
            scale = [jnp.zeros((8, LANES), jnp.float32) for g in tiles]
            for t in range(PIVOTS):
                g0, t0 = t // 8, t % 8
                pivot = over_rows(cols[t][g0], t0)
                r = pltpu.reciprocal(pivot, approx=True)
                r = r * (2.0 - pivot * r)
                f = {g: cols[t][g] * r for g in tiles if g >= g0}
                f[g0] = jnp.where(sub[g0] > t, f[g0], 0.0)
                scale[g0] = jnp.where(sub[g0] == t, lax.rsqrt(pivot), scale[g0])
                for u in range(t + 1, PIVOTS):
                    row = over_rows(cols[u][g0], t0)
                    for g in f:
                        cols[u][g] = cols[u][g] - f[g] * row
                d_row, e_row = over_rows(d[g0], t0), over_rows(e[g0], t0)
                for g in f:
                    d[g] = d[g] - f[g] * d_row
                    e[g] = e[g] - f[g] * e_row
            rows = pltpu.roll(jnp.concatenate([d[g] * scale[g] for g in tiles], axis=0), b * PIVOTS, 1)
            inverse = jnp.concatenate([e[g] * scale[g] for g in tiles], axis=0)
            later = jnp.where(lane >= b * PIVOTS + PIVOTS, rows, 0.0)
            ae[...] -= mm_tn_stacked(later, jnp.concatenate([rows, inverse], axis=1))
            ae[pl.ds(at, PIVOTS), LANES:] = inverse

    def exchange_begin(n):
        to_core(sx.at[n], sr.at[n], x_send.at[n], x_recv.at[n])
        pending.append((sr.at[n], x_send.at[n]))

    def reduce_1(n):
        to_xy(lambda p: part.at[n, pl.ds(pl.multiple_of(p * bi, 8), bi), :], r1.at[n, m], r1_send.at[n], r1_recv.at[n])
        pending.append((r1.at[n, pl.ds(0, nr - 1)], r1_send.at[n]))
        r1[n, m] = part[n, pl.ds(pl.multiple_of(m * bi, 8), bi), :]

    def reduce_2(n):
        wait(r1.at[n, pl.ds(0, nr - 1)], r1_recv.at[n])
        total = r1[n, 0]
        for k in range(1, nr):
            total = total + r1[n, k]
        s1[n] = total
        to_z(lambda p: s1.at[n], r2.at[n, z], r2_send.at[n], r2_recv.at[n])
        pending.append((r2.at[n, pl.ds(0, nz - 1)], r2_send.at[n]))
        r2[n, z] = total

    def reduce_3(n):
        wait(r2.at[n, pl.ds(0, nz - 1)], r2_recv.at[n])
        total = r2[n, 0]
        for k in range(1, nz):
            total = total + r2[n, k]
        s2[n] = total
        mine = pl.ds(pl.multiple_of(m * bi, 8), bi)
        to_xy(lambda p: s2.at[n], im.at[n, mine, :], r3_send.at[n], r3_recv.at[n])
        pending.append((im.at[n, pl.ds(0, (nr - 1) * bi), :], r3_send.at[n]))
        im[n, mine, :] = total

    def reduce_end(n):
        wait(im.at[n, pl.ds(0, (nr - 1) * bi), :], r3_recv.at[n])

    def unfolded():
        return jnp.concatenate([yb[0], yb[1]], axis=1)

    both = mm(f0t[...], unfolded())
    for p in range(2):
        sx[0, p] = both[:, p * LANES:(p + 1) * LANES]
    exchange_begin(0)
    wait(sr.at[0], x_recv.at[0])
    part[0] = mm_nt(unfolded(), jnp.concatenate([sx[0, p] + sr[0, p] for p in range(2)], axis=1))
    reduce_1(0)
    owned_z(0)
    yt[0] = yb[0].T
    reduce_2(0)
    ring_owned_xy()
    yt[1] = yb[1].T
    reduce_3(0)
    owned_z(1)
    reduce_end(0)

    sx[1] = mm(yt[...].reshape(2 * LANES, il), im[0]).reshape(2, LANES, LANES)
    exchange_begin(1)
    gx_s[0] = mm_tn(im[0], im[0])
    to_core(gx_s.at[0], gr.at[0], g_send.at[0], g_recv.at[0])
    pending.append((gr.at[0], g_send.at[0]))
    wait(sr.at[1], x_recv.at[1])
    part[1] = mm(unfolded(), (sx[1] + sr[1]).reshape(2 * LANES, LANES))
    reduce_1(1)
    owned_z(2)
    blocks = LANES // PIVOTS
    wait(gr.at[0], g_recv.at[0])
    chol_start(gx_s[0] + gr[0])
    chol_blocks(0, 3)
    reduce_2(1)
    owned_xy()
    chol_blocks(3, 6)
    reduce_3(1)
    ring_owned_z()
    chol_blocks(6, blocks)
    linv[...] = ae[:, LANES:]
    reduce_end(1)
    images = mm_nt(im[1], linv[...])
    gx_s[1] = mm_tn(images, images)
    to_core(gx_s.at[1], gr.at[1], g_send.at[1], g_recv.at[1])
    pending.append((gr.at[1], g_send.at[1]))

    owned_end()
    sx[2] = mm_tn(jnp.concatenate([yo[0], yo[1]], axis=1), images).reshape(2, LANES, LANES)
    exchange_begin(2)
    wait(gr.at[1], g_recv.at[1])
    chol_start(gx_s[1] + gr[1])
    chol_blocks(0, blocks)
    wait(sr.at[2], x_recv.at[2])
    for q in range(2):
        out_ref[:, q, :] = mm_nt(ae[:, LANES:], sx[2, q] + sr[2, q])
    finish()


def solution(mesh):
    nr, nz = mesh.shape["rad"], mesh.shape["span"]
    gx = 1
    while gx * gx < nr:
        gx *= 2

    def body(tensor, radial_factor, span_factor, start_factor):
        il = start_factor.shape[0]
        pb = il // nr - il // nr // 4
        zb = (il - nr * pb) // nz
        nc, ng, nq, nh = pb // CHUNK, pb // GROUP, zb // CHUNK, zb // GROUP
        bi = il // nr
        f32 = jnp.float32
        dma = pltpu.SemaphoreType.DMA
        vm = lambda *s: pltpu.VMEM(s, f32)
        scratch = [
            vm(*radial_factor.shape), vm(*span_factor.shape), vm(*start_factor.shape),
            vm(nc, nr, CHUNK * 16, LANES),
            vm(nr, 8, LANES), vm(nz, 8, LANES),
            vm(nz * 8, nr * 16), vm(nr * 16, nz * 64),
            vm(ng, nz, GROUP * 8, LANES), vm(ng, nz, GROUP * 8, LANES),
            vm(ng, nr, 2, GROUP, LANES),
            vm(2, il, LANES), vm(2, LANES, il), vm(LANES, il),
            vm(3, 2, LANES, LANES), vm(3, 2, LANES, LANES),
            vm(2, il, LANES),
            vm(2, nr, bi, LANES), vm(2, bi, LANES),
            vm(2, nz, bi, LANES), vm(2, bi, LANES),
            vm(2, il, LANES),
            vm(2, LANES, LANES), vm(2, LANES, LANES),
            vm(LANES, 2 * LANES), vm(LANES, LANES),
            vm(nz, 2, 2, pb, LANES), vm(2, il, LANES), vm(nr, zb, LANES),
            vm(nq, nz, CHUNK * 16, LANES), vm(nr * 8, nz * 32), vm(nz * 16, nr * 32),
            vm(nr, zb * 4, LANES), vm(nr, zb * 4, LANES), vm(nz * 2, zb, LANES),
            dma((6,)), dma((7, nc)),
            dma((2,)), dma((2,)),
            dma, dma((nc,)),
            dma, dma((nc,)),
            dma, dma,
            dma((3,)), dma((3,)),
            dma((2,)), dma((2,)),
            dma((2,)), dma((2,)), dma((2,)), dma((2,)), dma((2,)), dma((2,)),
            dma((4,)), dma((4,)),
            dma((3,)), dma((nq + 1,)), dma((nh,)),
        ]
        rows = tensor.reshape(il * 16, LANES)
        hbm = pl.BlockSpec(memory_space=pltpu.HBM)
        core = pl.pallas_call(
            functools.partial(kernel, nr, nz, gx),
            out_shape=jax.ShapeDtypeStruct((LANES, 2, LANES), f32),
            in_specs=[hbm] * 4,
            out_specs=pl.BlockSpec(memory_space=pltpu.VMEM),
            scratch_shapes=scratch,
            compiler_params=pltpu.CompilerParams(collective_id=0, has_side_effects=True, vmem_limit_bytes=62 * 1024 * 1024),
        )(rows, radial_factor, span_factor, start_factor)
        return core.reshape(LANES, 1, 2, LANES)

    in_specs = (P("ax", "rad", "span", None), P("rad", None), P("span", None), P("ax", None))
    out_specs = P(None, "rad", "span", None)
    return jax.shard_map(body, mesh=mesh, in_specs=in_specs, out_specs=out_specs, check_vma=False)
```

```python
import functools

import jax
import jax.numpy as jnp
from jax import lax
from jax.experimental import pallas as pl
from jax.experimental.pallas import tpu as pltpu
from jax.sharding import PartitionSpec as P

MESH = pl.DeviceIdType.MESH
HIGHEST = lax.Precision.HIGHEST
LANES = 128
CHUNK = 4
GROUP = 8
PIVOTS = 16


def mm(a, b):
    return lax.dot_general(a, b, (((1,), (0,)), ((), ())), precision=HIGHEST, preferred_element_type=jnp.float32)


def mm_nt(a, b):
    return lax.dot_general(a, b, (((1,), (1,)), ((), ())), precision=HIGHEST, preferred_element_type=jnp.float32)


def mm_tn(a, b):
    return lax.dot_general(a, b, (((0,), (0,)), ((), ())), precision=HIGHEST, preferred_element_type=jnp.float32)


def split3(x):
    high = x.astype(jnp.bfloat16)
    rest = x - high.astype(jnp.float32)
    mid = rest.astype(jnp.bfloat16)
    return high, mid, (rest - mid.astype(jnp.float32)).astype(jnp.bfloat16)


def mm_tn_stacked(a, b):
    ah, am, al = split3(a)
    bh, bm, bl = split3(b)
    left = jnp.concatenate([ah, ah, ah, am, am, al], axis=0)
    right = jnp.concatenate([bh, bm, bl, bh, bm, bh], axis=0)
    return lax.dot_general(left, right, (((0,), (0,)), ((), ())), preferred_element_type=jnp.float32)


def iota(shape, dim):
    return lax.broadcasted_iota(jnp.int32, shape, dim)


def kernel(nr, nz, gx, t_ref, a_ref, b_ref, f_ref, out_ref,
           av, bv, fv, xb, ag, bg, ma, mb, ub, wb, ysend, yb, yt, f0t,
           sx, sr, part, r1, s1, r2, s2, im, gx_s, gr, ae, linv, ya, yo, yd,
           xz, zm, rm, vs, vr, yz,
           in_sem, own_sem, ab_send, ab_recv, t_send, t_recv, w_send, w_recv, y_send, y_recv,
           x_send, x_recv, g_send, g_recv, r1_send, r1_recv, r2_send, r2_recv, r3_send, r3_recv,
           v_send, v_recv, q_send, q_recv, u_recv):
    c = lax.axis_index("ax")
    m = lax.axis_index("rad")
    z = lax.axis_index("span")
    gy = nr // gx
    rj, rk = 2 * nz, nr
    il = f_ref.shape[0]
    bi = il // nr
    pb = bi - bi // 4
    zb = (il - nr * pb) // nz
    nc, ng, per, nq = pb // CHUNK, pb // GROUP, GROUP // CHUNK, zb // CHUNK
    my, mx = m // gx, m % gx

    xs = [lax.rem(mx + d, gx) for d in range(gx)]
    ys = [lax.rem(my + d, gy) * gx for d in range(gy)]
    steps = [(dy, dx) for dy in range(gy) for dx in range(gx) if dy or dx]
    near_first = [ys[dy] + xs[dx] for dy, dx in steps]
    steps.sort(key=lambda s: -min(s[0], gy - s[0]) - min(s[1], gx - s[1]))
    xy_peers = [ys[dy] + xs[dx] for dy, dx in steps]
    z_peers = [lax.rem(z + d, nz) for d in sorted(range(1, nz), key=lambda d: -min(d, nz - d))]

    def remote(src, dst, send, recv, dev):
        return pltpu.make_async_remote_copy(src_ref=src, dst_ref=dst, send_sem=send, recv_sem=recv, device_id=dev, device_id_type=MESH)

    def to_xy(src_of, dst, send, recv, peers=xy_peers):
        for peer in peers:
            remote(src_of(peer), dst, send, recv, (c, peer, z)).start()

    def to_z(src_of, dst, send, recv):
        for peer in z_peers:
            remote(src_of(peer), dst, send, recv, (c, m, peer)).start()

    def to_core(src, dst, send, recv):
        remote(src, dst, send, recv, (1 - c, m, z)).start()

    def wait(view, sem):
        pltpu.make_async_copy(view, view, sem).wait()

    pending = []

    def finish():
        for view, sem in pending:
            wait(view, sem)

    arriving = [pltpu.make_async_copy(src, dst, in_sem.at[n]) for n, (src, dst) in enumerate(((a_ref, av), (b_ref, bv), (f_ref, fv)))]
    for copy in arriving:
        copy.start()

    barrier = pltpu.get_barrier_semaphore()

    def greet(dev):
        pl.semaphore_signal(barrier, inc=1, device_id=dev, device_id_type=MESH)

    for peer in xy_peers:
        greet((c, peer, z))
    for peer in z_peers:
        greet((c, m, peer))
    greet((1 - c, m, z))
    arriving[0].wait()
    arriving[1].wait()
    ag[m] = jnp.zeros((8, LANES), jnp.float32)
    ag[m, 0:4, 0:rj] = av[...]
    bg[z] = jnp.zeros((8, LANES), jnp.float32)
    bg[z, 0:4, 0:rk] = bv[...]
    pl.semaphore_wait(barrier, (nr - 1) + (nz - 1) + 1)

    def t_rows(peer, k):
        return t_ref.at[pl.ds(pl.multiple_of((peer * pb + k * CHUNK) * 16, CHUNK * 16), CHUNK * 16), :]

    def t_ring(peer, k):
        return t_ref.at[pl.ds(pl.multiple_of((nr * pb + peer * zb + k * CHUNK) * 16, CHUNK * 16), CHUNK * 16), :]

    def to_plane(k):
        pltpu.make_async_copy(t_rows(m, k), xb.at[k, m], own_sem.at[0, k]).start()
        to_xy(lambda p: t_rows(p, k), xb.at[k, m], t_send, t_recv.at[k])

    def to_ring(k):
        pltpu.make_async_copy(t_ring(z, k), xz.at[k, z], own_sem.at[4, k]).start()
        to_z(lambda p: t_ring(p, k), xz.at[k, z], q_send.at[0], q_recv.at[k])

    to_ring(0)
    to_plane(0)
    to_xy(lambda p: ag.at[m], ag.at[m], ab_send.at[0], ab_recv.at[0])
    pending.append((ag.at[pl.ds(0, nr - 1)], ab_send.at[0]))
    to_z(lambda p: bg.at[z], bg.at[z], ab_send.at[1], ab_recv.at[1])
    pending.append((bg.at[pl.ds(0, nz - 1)], ab_send.at[1]))

    @pl.loop(1, nq)
    def _(k):
        to_ring(k)
        to_plane(k)

    @pl.loop(nq, nc)
    def _(k):
        to_plane(k)

    pending.append((xb.at[:, pl.ds(0, nr - 1)], t_send))
    pending.append((xz.at[:, pl.ds(0, nz - 1)], q_send.at[0]))
    arriving[2].wait()
    f0t[...] = fv[...].T

    wait(ag.at[pl.ds(0, nr - 1)], ab_recv.at[0])
    wait(bg.at[pl.ds(0, nz - 1)], ab_recv.at[1])

    def spread(gathered, shape, row_div, col_div, col_of, same):
        rows, cols = shape
        n = gathered.shape[0] * 8
        pick = (iota((rows, LANES), 0) // row_div == iota((rows, LANES), 1)).astype(jnp.float32)
        at, col = iota((n, cols), 0), iota((n, cols), 1)
        place = (at == (col // col_div) * 8 + col_of(col)).astype(jnp.float32)
        full = mm(mm_nt(pick, gathered[...].reshape(n, LANES)), place)
        return jnp.where(same(iota(shape, 0), iota(shape, 1)), full, 0.0)

    ma[...] = spread(ag, ma.shape, 4, 16, lambda col: (col % 16) // 4, lambda r, col: r % 4 == col % 4)
    mb[...] = spread(bg, mb.shape, 16, 64, lambda col: col % 4, lambda r, col: jnp.logical_and(
        (r // 8) % 2 == (col // 4) % 2, r % 8 == (col // 8) % 8))
    zm[...] = spread(bg, zm.shape, 8, 32, lambda col: col % 4, lambda r, col: r % 8 == (col // 4) % 8)
    rm[...] = spread(ag, rm.shape, 8, 32, lambda col: col % 4, lambda r, col: r % 8 == (col // 4) % 8)

    def radial(k):
        wait(xb.at[k, pl.ds(0, nr - 1)], t_recv.at[k])
        wait(xb.at[k, 0], own_sem.at[0, k])

        for h in range(CHUNK // 2):
            both = xb[k, :, pl.ds(h * 32, 32), :]
            x0 = both[:, 0:16, :].reshape(nr * 16, LANES)
            x1 = both[:, 16:32, :].reshape(nr * 16, LANES)
            u = mm(ma[...], jnp.concatenate([x0, x1], axis=1))
            at = (k % per) * CHUNK * 8 + h * 16
            ub[k // per, :, pl.ds(at, 8), :] = u[:, 0:LANES].reshape(nz, 8, LANES)
            ub[k // per, :, pl.ds(at + 8, 8), :] = u[:, LANES:].reshape(nz, 8, LANES)

        g, half = k // per, pl.ds((k % per) * CHUNK * 8, CHUNK * 8)
        pltpu.make_async_copy(ub.at[g, z, half], wb.at[g, z, half], own_sem.at[1, k]).start()
        to_z(lambda p: ub.at[g, p, half], wb.at[g, z, half], w_send, w_recv.at[k])

    def y_rows(g):
        return yb.at[:, pl.ds(pl.multiple_of(m * pb + g * GROUP, 8), GROUP), :]

    def span(g):
        for h in range(per):
            wait(wb.at[g, pl.ds(0, nz - 1), pl.ds(0, CHUNK * 8)], w_recv.at[g * per + h])
            wait(wb.at[g, 0, pl.ds(0, CHUNK * 8)], own_sem.at[1, g * per + h])
        y = mm(mb[...], wb[g].reshape(nz * 64, LANES))
        ysend[g] = y.reshape(nr, 2, GROUP, LANES)
        pltpu.make_async_copy(ysend.at[g, m], y_rows(g), own_sem.at[2, g]).start()
        to_xy(lambda p: ysend.at[g, p], y_rows(g), y_send, y_recv)

    def ring_span(k):
        wait(xz.at[k, pl.ds(0, nz - 1)], q_recv.at[k])
        wait(xz.at[k, 0], own_sem.at[4, k])
        for h in range(CHUNK // 2):
            rows = xz[k, :, pl.ds(h * 32, 32), :].reshape(nz * 32, LANES)
            vs[:, pl.ds((k * (CHUNK // 2) + h) * 8, 8), :] = mm(zm[...], rows).reshape(nr, 8, LANES)
        if k % per == per - 1:
            rows = pl.ds((k // per) * GROUP * 4, GROUP * 4)
            pltpu.make_async_copy(vs.at[m, rows], vr.at[m, rows], own_sem.at[5, k // per]).start()
            to_xy(lambda p: vs.at[p, rows], vr.at[m, rows], q_send.at[1], u_recv.at[k // per])

    def ring_y(g):
        return yb.at[:, pl.ds(pl.multiple_of(nr * pb + z * zb + g * GROUP, 8), GROUP), :]

    def ring_radial(g):
        rows, part_rows = pl.ds(g * GROUP * 4, GROUP * 4), pl.ds(g * GROUP, GROUP)
        wait(vr.at[pl.ds(0, nr - 1), rows], u_recv.at[g])
        wait(vr.at[0, rows], own_sem.at[5, g])
        y = mm(rm[...], vr[:, rows, :].reshape(nr * 32, LANES))
        yz[:, part_rows, :] = y.reshape(rj, GROUP, LANES)
        pltpu.make_async_copy(yz.at[pl.ds(2 * z, 2), part_rows], ring_y(g), own_sem.at[6, g]).start()
        to_z(lambda p: yz.at[pl.ds(2 * p, 2), part_rows], ring_y(g), q_send.at[2], q_recv.at[nq])

    spans = rings = 0
    for k in range(nc):
        radial(k)
        if k % per == per // 2 and k > per:
            span(spans)
            spans += 1
        while rings < nq and rings * (nc - 1) < k * nq:
            ring_span(rings)
            rings += 1
    ring_radial(0)
    span(ng - 1)
    for g in range(1, zb // GROUP):
        ring_radial(g)
    pending.extend([(wb.at[:, pl.ds(0, nz - 1)], w_send), (ysend.at[:, pl.ds(0, nr - 1)], y_send)])
    pending.extend([(vr.at[pl.ds(0, nr - 1)], q_send.at[1]), (yb.at[:, pl.ds(0, (nz - 1) * zb), :], q_send.at[2])])
    wait(yb.at[:, pl.ds(0, (nr - 1) * pb), :], y_recv)
    wait(yb.at[:, pl.ds(0, (nz - 1) * zb), :], q_recv.at[nq])
    for g in range(ng):
        wait(ysend.at[0, 0], own_sem.at[2, g])
    for g in range(zb // GROUP):
        wait(yz.at[pl.ds(0, 2), pl.ds(0, GROUP)], own_sem.at[6, g])

    def owned_z(g):
        owned = ya.at[z, :, :, pl.ds(g * GROUP, GROUP), :]
        pltpu.make_async_copy(ysend.at[g, pl.ds(2 * z, 2)], owned, own_sem.at[3, g]).start()
        to_z(lambda p: ysend.at[g, pl.ds(2 * p, 2)], owned, v_send.at[0], v_recv.at[0])

    def owned_xy():
        pending.append((ya.at[pl.ds(0, nz - 1)], v_send.at[0]))
        wait(ya.at[pl.ds(0, nz - 1)], v_recv.at[0])
        for g in range(ng):
            wait(ysend.at[0, pl.ds(0, 2)], own_sem.at[3, g])
        owned = yo.at[:, pl.ds(pl.multiple_of(m * pb, 8), pb), :]
        pltpu.make_async_copy(ya.at[m // 2, :, m % 2], owned, in_sem.at[3]).start()
        to_xy(lambda p: ya.at[p // 2, :, p % 2], owned, v_send.at[1], v_recv.at[1])
        pending.append((yo.at[:, pl.ds(0, (nr - 1) * pb), :], v_send.at[1]))

    def ring_owned_xy():
        pltpu.make_async_copy(yz.at[m], yd.at[m], in_sem.at[4]).start()
        to_xy(lambda p: yz.at[p], yd.at[m], v_send.at[2], v_recv.at[2])
        pending.append((yd.at[pl.ds(0, nr - 1)], v_send.at[2]))

    def ring_owned_z():
        wait(yd.at[pl.ds(0, nr - 1)], v_recv.at[2])
        wait(yd.at[0], in_sem.at[4])
        owned = yo.at[:, pl.ds(pl.multiple_of(nr * pb + z * zb, 8), zb), :]
        pltpu.make_async_copy(yd.at[pl.ds(2 * z, 2)], owned, in_sem.at[5]).start()
        to_z(lambda p: yd.at[pl.ds(2 * p, 2)], owned, v_send.at[3], v_recv.at[3])
        pending.append((yo.at[:, pl.ds(0, (nz - 1) * zb), :], v_send.at[3]))

    def owned_end():
        wait(yo.at[:, pl.ds(0, (nr - 1) * pb), :], v_recv.at[1])
        wait(ya.at[0, :, 0], in_sem.at[3])
        wait(yo.at[:, pl.ds(0, (nz - 1) * zb), :], v_recv.at[3])
        wait(yd.at[pl.ds(0, 2)], in_sem.at[5])

    def chol_start(gram):
        ae[:, 0:LANES] = gram
        eye = iota((LANES, LANES), 0) == iota((LANES, LANES), 1)
        ae[:, LANES:] = eye.astype(jnp.float32)

    tiles = range(PIVOTS // 8)
    sub = [iota((8, LANES), 0) + 8 * g for g in tiles]
    lane = iota((PIVOTS, LANES), 1)

    def over_rows(x, t):
        return jnp.broadcast_to(x[t:t + 1, :], (8, LANES))

    def chol_blocks(lo, hi):
        @pl.loop(lo, hi)
        def _(b):
            at = pl.multiple_of(b * PIVOTS, PIVOTS)
            turned = pltpu.roll(ae[pl.ds(at, PIVOTS), 0:LANES], (LANES - b * PIVOTS) % LANES, 1)
            d = [turned[8 * g:8 * g + 8] for g in tiles]
            e = [ae[pl.ds(at + 8 * g, 8), LANES:] for g in tiles]
            cols = [[jnp.broadcast_to(d[g][:, t:t + 1], (8, LANES)) for g in tiles] for t in range(PIVOTS)]
            scale = [jnp.zeros((8, LANES), jnp.float32) for g in tiles]
            for t in range(PIVOTS):
                g0, t0 = t // 8, t % 8
                pivot = over_rows(cols[t][g0], t0)
                r = pltpu.reciprocal(pivot, approx=True)
                r = r * (2.0 - pivot * r)
                f = {g: cols[t][g] * r for g in tiles if g >= g0}
                f[g0] = jnp.where(sub[g0] > t, f[g0], 0.0)
                scale[g0] = jnp.where(sub[g0] == t, lax.rsqrt(pivot), scale[g0])
                for u in range(t + 1, PIVOTS):
                    row = over_rows(cols[u][g0], t0)
                    for g in f:
                        cols[u][g] = cols[u][g] - f[g] * row
                d_row, e_row = over_rows(d[g0], t0), over_rows(e[g0], t0)
                for g in f:
                    d[g] = d[g] - f[g] * d_row
                    e[g] = e[g] - f[g] * e_row
            rows = pltpu.roll(jnp.concatenate([d[g] * scale[g] for g in tiles], axis=0), b * PIVOTS, 1)
            inverse = jnp.concatenate([e[g] * scale[g] for g in tiles], axis=0)
            later = jnp.where(lane >= b * PIVOTS + PIVOTS, rows, 0.0)
            ae[...] -= mm_tn_stacked(later, jnp.concatenate([rows, inverse], axis=1))
            ae[pl.ds(at, PIVOTS), LANES:] = inverse

    def exchange_begin(n):
        to_core(sx.at[n], sr.at[n], x_send.at[n], x_recv.at[n])
        pending.append((sr.at[n], x_send.at[n]))

    def reduce_1(n, product):
        for dy in sorted(range(gy), key=lambda d: -min(d, gy - d)):
            block = pl.ds(pl.multiple_of(ys[dy] * bi, 8), gx * bi)
            part[n, block, :] = product(jnp.concatenate([yb[0, block, :], yb[1, block, :]], axis=1))
            peers = [ys[dy] + xs[dx] for dx in sorted(range(gx), key=lambda d: -min(d, gx - d)) if dx or dy]
            to_xy(lambda p: part.at[n, pl.ds(pl.multiple_of(p * bi, 8), bi), :], r1.at[n, m], r1_send.at[n], r1_recv.at[n], peers)
        pending.append((r1.at[n, pl.ds(0, nr - 1)], r1_send.at[n]))
        r1[n, m] = part[n, pl.ds(pl.multiple_of(m * bi, 8), bi), :]

    def reduce_2(n):
        wait(r1.at[n, pl.ds(0, nr - 1)], r1_recv.at[n])
        total = r1[n, 0]
        for k in range(1, nr):
            total = total + r1[n, k]
        s1[n] = total
        to_z(lambda p: s1.at[n], r2.at[n, z], r2_send.at[n], r2_recv.at[n])
        pending.append((r2.at[n, pl.ds(0, nz - 1)], r2_send.at[n]))
        r2[n, z] = total

    def reduce_3(n):
        wait(r2.at[n, pl.ds(0, nz - 1)], r2_recv.at[n])
        total = r2[n, 0]
        for k in range(1, nz):
            total = total + r2[n, k]
        s2[n] = total
        mine = pl.ds(pl.multiple_of(m * bi, 8), bi)
        to_xy(lambda p: s2.at[n], im.at[n, mine, :], r3_send.at[n], r3_recv.at[n])
        pending.append((im.at[n, pl.ds(0, (nr - 1) * bi), :], r3_send.at[n]))
        im[n, mine, :] = total

    def reduce_end(n):
        wait(im.at[n, pl.ds(0, (nr - 1) * bi), :], r3_recv.at[n])

    def unfolded():
        return jnp.concatenate([yb[0], yb[1]], axis=1)

    both = mm(f0t[...], unfolded())
    for p in range(2):
        sx[0, p] = both[:, p * LANES:(p + 1) * LANES]
    exchange_begin(0)
    wait(sr.at[0], x_recv.at[0])
    small = jnp.concatenate([sx[0, p] + sr[0, p] for p in range(2)], axis=1)
    reduce_1(0, lambda rows: mm_nt(rows, small))
    owned_z(0)
    yt[0] = yb[0].T
    reduce_2(0)
    ring_owned_xy()
    yt[1] = yb[1].T
    reduce_3(0)
    owned_z(1)
    reduce_end(0)

    sx[1] = mm(yt[...].reshape(2 * LANES, il), im[0]).reshape(2, LANES, LANES)
    exchange_begin(1)
    gx_s[0] = mm_tn(im[0], im[0])
    to_core(gx_s.at[0], gr.at[0], g_send.at[0], g_recv.at[0])
    pending.append((gr.at[0], g_send.at[0]))
    wait(sr.at[1], x_recv.at[1])
    small = (sx[1] + sr[1]).reshape(2 * LANES, LANES)
    reduce_1(1, lambda rows: mm(rows, small))
    owned_z(2)
    blocks = LANES // PIVOTS
    wait(gr.at[0], g_recv.at[0])
    chol_start(gx_s[0] + gr[0])
    chol_blocks(0, 3)
    reduce_2(1)
    owned_xy()
    chol_blocks(3, 6)
    reduce_3(1)
    ring_owned_z()
    chol_blocks(6, blocks)
    linv[...] = ae[:, LANES:]
    reduce_end(1)
    images = mm_nt(im[1], linv[...])
    gx_s[1] = mm_tn(images, images)
    to_core(gx_s.at[1], gr.at[1], g_send.at[1], g_recv.at[1])
    pending.append((gr.at[1], g_send.at[1]))

    owned_end()
    sx[2] = mm_tn(jnp.concatenate([yo[0], yo[1]], axis=1), images).reshape(2, LANES, LANES)
    exchange_begin(2)
    wait(gr.at[1], g_recv.at[1])
    chol_start(gx_s[1] + gr[1])
    chol_blocks(0, blocks)
    wait(sr.at[2], x_recv.at[2])
    for q in range(2):
        out_ref[:, q, :] = mm_nt(ae[:, LANES:], sx[2, q] + sr[2, q])
    finish()


def solution(mesh):
    nr, nz = mesh.shape["rad"], mesh.shape["span"]
    gx = 1
    while gx * gx < nr:
        gx *= 2

    def body(tensor, radial_factor, span_factor, start_factor):
        il = start_factor.shape[0]
        pb = il // nr - il // nr // 4
        zb = (il - nr * pb) // nz
        nc, ng, nq, nh = pb // CHUNK, pb // GROUP, zb // CHUNK, zb // GROUP
        bi = il // nr
        f32 = jnp.float32
        dma = pltpu.SemaphoreType.DMA
        vm = lambda *s: pltpu.VMEM(s, f32)
        scratch = [
            vm(*radial_factor.shape), vm(*span_factor.shape), vm(*start_factor.shape),
            vm(nc, nr, CHUNK * 16, LANES),
            vm(nr, 8, LANES), vm(nz, 8, LANES),
            vm(nz * 8, nr * 16), vm(nr * 16, nz * 64),
            vm(ng, nz, GROUP * 8, LANES), vm(ng, nz, GROUP * 8, LANES),
            vm(ng, nr, 2, GROUP, LANES),
            vm(2, il, LANES), vm(2, LANES, il), vm(LANES, il),
            vm(3, 2, LANES, LANES), vm(3, 2, LANES, LANES),
            vm(2, il, LANES),
            vm(2, nr, bi, LANES), vm(2, bi, LANES),
            vm(2, nz, bi, LANES), vm(2, bi, LANES),
            vm(2, il, LANES),
            vm(2, LANES, LANES), vm(2, LANES, LANES),
            vm(LANES, 2 * LANES), vm(LANES, LANES),
            vm(nz, 2, 2, pb, LANES), vm(2, il, LANES), vm(nr, zb, LANES),
            vm(nq, nz, CHUNK * 16, LANES), vm(nr * 8, nz * 32), vm(nz * 16, nr * 32),
            vm(nr, zb * 4, LANES), vm(nr, zb * 4, LANES), vm(nz * 2, zb, LANES),
            dma((6,)), dma((7, nc)),
            dma((2,)), dma((2,)),
            dma, dma((nc,)),
            dma, dma((nc,)),
            dma, dma,
            dma((3,)), dma((3,)),
            dma((2,)), dma((2,)),
            dma((2,)), dma((2,)), dma((2,)), dma((2,)), dma((2,)), dma((2,)),
            dma((4,)), dma((4,)),
            dma((3,)), dma((nq + 1,)), dma((nh,)),
        ]
        rows = tensor.reshape(il * 16, LANES)
        hbm = pl.BlockSpec(memory_space=pltpu.HBM)
        core = pl.pallas_call(
            functools.partial(kernel, nr, nz, gx),
            out_shape=jax.ShapeDtypeStruct((LANES, 2, LANES), f32),
            in_specs=[hbm] * 4,
            out_specs=pl.BlockSpec(memory_space=pltpu.VMEM),
            scratch_shapes=scratch,
            compiler_params=pltpu.CompilerParams(collective_id=0, has_side_effects=True, vmem_limit_bytes=62 * 1024 * 1024),
        )(rows, radial_factor, span_factor, start_factor)
        return core.reshape(LANES, 1, 2, LANES)

    in_specs = (P("ax", "rad", "span", None), P("rad", None), P("span", None), P("ax", None))
    out_specs = P(None, "rad", "span", None)
    return jax.shard_map(body, mesh=mesh, in_specs=in_specs, out_specs=out_specs, check_vma=False)
```

```python
import functools

import jax
import jax.numpy as jnp
from jax import lax
from jax.experimental import pallas as pl
from jax.experimental.pallas import tpu as pltpu
from jax.sharding import PartitionSpec as P

MESH = pl.DeviceIdType.MESH
HIGHEST = lax.Precision.HIGHEST
LANES = 128
CHUNK = 4
GROUP = 8
PIVOTS = 32


def mm(a, b):
    return lax.dot_general(a, b, (((1,), (0,)), ((), ())), precision=HIGHEST, preferred_element_type=jnp.float32)


def mm_nt(a, b):
    return lax.dot_general(a, b, (((1,), (1,)), ((), ())), precision=HIGHEST, preferred_element_type=jnp.float32)


def mm_tn(a, b):
    return lax.dot_general(a, b, (((0,), (0,)), ((), ())), precision=HIGHEST, preferred_element_type=jnp.float32)


def split3(x):
    high = x.astype(jnp.bfloat16)
    rest = x - high.astype(jnp.float32)
    mid = rest.astype(jnp.bfloat16)
    return high, mid, (rest - mid.astype(jnp.float32)).astype(jnp.bfloat16)


def split2(x):
    high = x.astype(jnp.bfloat16)
    return high, (x - high.astype(jnp.float32)).astype(jnp.bfloat16)


def mm3(a, b, dims=((1,), (0,))):
    ah, al = split2(a)
    bh, bl = split2(b)
    one = lambda x, y: lax.dot_general(x, y, (dims, ((), ())), preferred_element_type=jnp.float32)
    return one(ah, bh) + (one(ah, bl) + one(al, bh))


def mm_tn_stacked(a, b):
    ah, am, al = split3(a)
    bh, bm, bl = split3(b)
    left = jnp.concatenate([ah, ah, ah, am, am, al], axis=0)
    right = jnp.concatenate([bh, bm, bl, bh, bm, bh], axis=0)
    return lax.dot_general(left, right, (((0,), (0,)), ((), ())), preferred_element_type=jnp.float32)


def iota(shape, dim):
    return lax.broadcasted_iota(jnp.int32, shape, dim)


def kernel(nr, nz, gx, t_ref, a_ref, b_ref, f_ref, out_ref,
           av, bv, fv, xb, ag, bg, ma, mb, ub, wb, ysend, yb, yt, f0t,
           sx, sr, part, r1, s1, r2, s2, im, gx_s, gr, ae, linv, ya, yo, yd,
           xz, zm, rm, vs, vr, yz,
           in_sem, own_sem, ab_send, ab_recv, t_send, t_recv, w_send, w_recv, y_send, y_recv,
           x_send, x_recv, g_send, g_recv, r1_send, r1_recv, r2_send, r2_recv, r3_send, r3_recv,
           v_send, v_recv, q_send, q_recv, u_recv):
    c = lax.axis_index("ax")
    m = lax.axis_index("rad")
    z = lax.axis_index("span")
    gy = nr // gx
    rj, rk = 2 * nz, nr
    il = f_ref.shape[0]
    bi = il // nr
    pb = bi - bi // 4
    zb = (il - nr * pb) // nz
    nc, ng, per, nq = pb // CHUNK, pb // GROUP, GROUP // CHUNK, zb // CHUNK
    my, mx = m // gx, m % gx

    xs = [lax.rem(mx + d, gx) for d in range(gx)]
    ys = [lax.rem(my + d, gy) * gx for d in range(gy)]
    steps = [(dy, dx) for dy in range(gy) for dx in range(gx) if dy or dx]
    near_first = [ys[dy] + xs[dx] for dy, dx in steps]
    steps.sort(key=lambda s: -min(s[0], gy - s[0]) - min(s[1], gx - s[1]))
    xy_peers = [ys[dy] + xs[dx] for dy, dx in steps]
    z_peers = [lax.rem(z + d, nz) for d in sorted(range(1, nz), key=lambda d: -min(d, nz - d))]

    def remote(src, dst, send, recv, dev):
        return pltpu.make_async_remote_copy(src_ref=src, dst_ref=dst, send_sem=send, recv_sem=recv, device_id=dev, device_id_type=MESH)

    def to_xy(src_of, dst, send, recv, peers=xy_peers):
        for peer in peers:
            remote(src_of(peer), dst, send, recv, (c, peer, z)).start()

    def to_z(src_of, dst, send, recv):
        for peer in z_peers:
            remote(src_of(peer), dst, send, recv, (c, m, peer)).start()

    def to_core(src, dst, send, recv):
        remote(src, dst, send, recv, (1 - c, m, z)).start()

    def wait(view, sem):
        pltpu.make_async_copy(view, view, sem).wait()

    pending = []

    def finish():
        for view, sem in pending:
            wait(view, sem)

    arriving = [pltpu.make_async_copy(src, dst, in_sem.at[n]) for n, (src, dst) in enumerate(((a_ref, av), (b_ref, bv), (f_ref, fv)))]
    for copy in arriving:
        copy.start()

    barrier = pltpu.get_barrier_semaphore()

    def greet(dev):
        pl.semaphore_signal(barrier, inc=1, device_id=dev, device_id_type=MESH)

    for peer in xy_peers:
        greet((c, peer, z))
    for peer in z_peers:
        greet((c, m, peer))
    greet((1 - c, m, z))
    arriving[0].wait()
    arriving[1].wait()
    ag[m] = jnp.zeros((8, LANES), jnp.float32)
    ag[m, 0:4, 0:rj] = av[...]
    bg[z] = jnp.zeros((8, LANES), jnp.float32)
    bg[z, 0:4, 0:rk] = bv[...]
    pl.semaphore_wait(barrier, (nr - 1) + (nz - 1) + 1)

    def t_rows(peer, k):
        return t_ref.at[pl.ds(pl.multiple_of((peer * pb + k * CHUNK) * 16, CHUNK * 16), CHUNK * 16), :]

    def t_ring(peer, k):
        return t_ref.at[pl.ds(pl.multiple_of((nr * pb + peer * zb + k * CHUNK) * 16, CHUNK * 16), CHUNK * 16), :]

    def to_plane(k):
        pltpu.make_async_copy(t_rows(m, k), xb.at[k, m], own_sem.at[0, k]).start()
        to_xy(lambda p: t_rows(p, k), xb.at[k, m], t_send, t_recv.at[k])

    def to_ring(k):
        pltpu.make_async_copy(t_ring(z, k), xz.at[k, z], own_sem.at[4, k]).start()
        to_z(lambda p: t_ring(p, k), xz.at[k, z], q_send.at[0], q_recv.at[k])

    to_ring(0)
    to_plane(0)
    to_xy(lambda p: ag.at[m], ag.at[m], ab_send.at[0], ab_recv.at[0])
    pending.append((ag.at[pl.ds(0, nr - 1)], ab_send.at[0]))
    to_z(lambda p: bg.at[z], bg.at[z], ab_send.at[1], ab_recv.at[1])
    pending.append((bg.at[pl.ds(0, nz - 1)], ab_send.at[1]))

    @pl.loop(1, nq)
    def _(k):
        to_ring(k)
        to_plane(k)

    @pl.loop(nq, nc)
    def _(k):
        to_plane(k)

    pending.append((xb.at[:, pl.ds(0, nr - 1)], t_send))
    pending.append((xz.at[:, pl.ds(0, nz - 1)], q_send.at[0]))
    arriving[2].wait()
    f0t[...] = fv[...].T

    wait(ag.at[pl.ds(0, nr - 1)], ab_recv.at[0])
    wait(bg.at[pl.ds(0, nz - 1)], ab_recv.at[1])

    def spread(gathered, shape, row_div, col_div, col_of, same):
        rows, cols = shape
        n = gathered.shape[0] * 8
        pick = (iota((rows, LANES), 0) // row_div == iota((rows, LANES), 1)).astype(jnp.float32)
        at, col = iota((n, cols), 0), iota((n, cols), 1)
        place = (at == (col // col_div) * 8 + col_of(col)).astype(jnp.float32)
        full = mm(mm_nt(pick, gathered[...].reshape(n, LANES)), place)
        return jnp.where(same(iota(shape, 0), iota(shape, 1)), full, 0.0)

    ma[...] = spread(ag, ma.shape, 4, 16, lambda col: (col % 16) // 4, lambda r, col: r % 4 == col % 4)
    mb[...] = spread(bg, mb.shape, 16, 64, lambda col: col % 4, lambda r, col: jnp.logical_and(
        (r // 8) % 2 == (col // 4) % 2, r % 8 == (col // 8) % 8))
    zm[...] = spread(bg, zm.shape, 8, 32, lambda col: col % 4, lambda r, col: r % 8 == (col // 4) % 8)
    rm[...] = spread(ag, rm.shape, 8, 32, lambda col: col % 4, lambda r, col: r % 8 == (col // 4) % 8)

    def radial(k):
        wait(xb.at[k, pl.ds(0, nr - 1)], t_recv.at[k])
        wait(xb.at[k, 0], own_sem.at[0, k])

        for h in range(CHUNK // 2):
            both = xb[k, :, pl.ds(h * 32, 32), :]
            x0 = both[:, 0:16, :].reshape(nr * 16, LANES)
            x1 = both[:, 16:32, :].reshape(nr * 16, LANES)
            u = mm3(ma[...], jnp.concatenate([x0, x1], axis=1))
            at = (k % per) * CHUNK * 8 + h * 16
            ub[k // per, :, pl.ds(at, 8), :] = u[:, 0:LANES].reshape(nz, 8, LANES)
            ub[k // per, :, pl.ds(at + 8, 8), :] = u[:, LANES:].reshape(nz, 8, LANES)

        g, half = k // per, pl.ds((k % per) * CHUNK * 8, CHUNK * 8)
        pltpu.make_async_copy(ub.at[g, z, half], wb.at[g, z, half], own_sem.at[1, k]).start()
        to_z(lambda p: ub.at[g, p, half], wb.at[g, z, half], w_send, w_recv.at[k])

    def y_rows(g):
        return yb.at[:, pl.ds(pl.multiple_of(m * pb + g * GROUP, 8), GROUP), :]

    def span(g):
        for h in range(per):
            wait(wb.at[g, pl.ds(0, nz - 1), pl.ds(0, CHUNK * 8)], w_recv.at[g * per + h])
            wait(wb.at[g, 0, pl.ds(0, CHUNK * 8)], own_sem.at[1, g * per + h])
        y = mm3(mb[...], wb[g].reshape(nz * 64, LANES))
        ysend[g] = y.reshape(nr, 2, GROUP, LANES)
        pltpu.make_async_copy(ysend.at[g, m], y_rows(g), own_sem.at[2, g]).start()
        to_xy(lambda p: ysend.at[g, p], y_rows(g), y_send, y_recv)

    def ring_span(k):
        wait(xz.at[k, pl.ds(0, nz - 1)], q_recv.at[k])
        wait(xz.at[k, 0], own_sem.at[4, k])
        for h in range(CHUNK // 2):
            rows = xz[k, :, pl.ds(h * 32, 32), :].reshape(nz * 32, LANES)
            vs[:, pl.ds((k * (CHUNK // 2) + h) * 8, 8), :] = mm3(zm[...], rows).reshape(nr, 8, LANES)
        if k % per == per - 1:
            rows = pl.ds((k // per) * GROUP * 4, GROUP * 4)
            pltpu.make_async_copy(vs.at[m, rows], vr.at[m, rows], own_sem.at[5, k // per]).start()
            to_xy(lambda p: vs.at[p, rows], vr.at[m, rows], q_send.at[1], u_recv.at[k // per])

    def ring_y(g):
        return yb.at[:, pl.ds(pl.multiple_of(nr * pb + z * zb + g * GROUP, 8), GROUP), :]

    def ring_radial(g):
        rows, part_rows = pl.ds(g * GROUP * 4, GROUP * 4), pl.ds(g * GROUP, GROUP)
        wait(vr.at[pl.ds(0, nr - 1), rows], u_recv.at[g])
        wait(vr.at[0, rows], own_sem.at[5, g])
        y = mm3(rm[...], vr[:, rows, :].reshape(nr * 32, LANES))
        yz[:, part_rows, :] = y.reshape(rj, GROUP, LANES)
        pltpu.make_async_copy(yz.at[pl.ds(2 * z, 2), part_rows], ring_y(g), own_sem.at[6, g]).start()
        to_z(lambda p: yz.at[pl.ds(2 * p, 2), part_rows], ring_y(g), q_send.at[2], q_recv.at[nq])

    spans = rings = 0
    for k in range(nc):
        radial(k)
        if k % per == per // 2 and k > per:
            span(spans)
            spans += 1
        while rings < nq and rings * (nc - 1) < k * nq:
            ring_span(rings)
            rings += 1
    ring_radial(0)
    span(ng - 1)
    for g in range(1, zb // GROUP):
        ring_radial(g)
    pending.extend([(wb.at[:, pl.ds(0, nz - 1)], w_send), (ysend.at[:, pl.ds(0, nr - 1)], y_send)])
    pending.extend([(vr.at[pl.ds(0, nr - 1)], q_send.at[1]), (yb.at[:, pl.ds(0, (nz - 1) * zb), :], q_send.at[2])])
    wait(yb.at[:, pl.ds(0, (nr - 1) * pb), :], y_recv)
    wait(yb.at[:, pl.ds(0, (nz - 1) * zb), :], q_recv.at[nq])
    for g in range(ng):
        wait(ysend.at[0, 0], own_sem.at[2, g])
    for g in range(zb // GROUP):
        wait(yz.at[pl.ds(0, 2), pl.ds(0, GROUP)], own_sem.at[6, g])

    def owned_z(g):
        owned = ya.at[z, :, :, pl.ds(g * GROUP, GROUP), :]
        pltpu.make_async_copy(ysend.at[g, pl.ds(2 * z, 2)], owned, own_sem.at[3, g]).start()
        to_z(lambda p: ysend.at[g, pl.ds(2 * p, 2)], owned, v_send.at[0], v_recv.at[0])

    def owned_xy():
        pending.append((ya.at[pl.ds(0, nz - 1)], v_send.at[0]))
        wait(ya.at[pl.ds(0, nz - 1)], v_recv.at[0])
        for g in range(ng):
            wait(ysend.at[0, pl.ds(0, 2)], own_sem.at[3, g])
        owned = yo.at[:, pl.ds(pl.multiple_of(m * pb, 8), pb), :]
        pltpu.make_async_copy(ya.at[m // 2, :, m % 2], owned, in_sem.at[3]).start()
        to_xy(lambda p: ya.at[p // 2, :, p % 2], owned, v_send.at[1], v_recv.at[1])
        pending.append((yo.at[:, pl.ds(0, (nr - 1) * pb), :], v_send.at[1]))

    def ring_owned_xy():
        pltpu.make_async_copy(yz.at[m], yd.at[m], in_sem.at[4]).start()
        to_xy(lambda p: yz.at[p], yd.at[m], v_send.at[2], v_recv.at[2])
        pending.append((yd.at[pl.ds(0, nr - 1)], v_send.at[2]))

    def ring_owned_z():
        wait(yd.at[pl.ds(0, nr - 1)], v_recv.at[2])
        wait(yd.at[0], in_sem.at[4])
        owned = yo.at[:, pl.ds(pl.multiple_of(nr * pb + z * zb, 8), zb), :]
        pltpu.make_async_copy(yd.at[pl.ds(2 * z, 2)], owned, in_sem.at[5]).start()
        to_z(lambda p: yd.at[pl.ds(2 * p, 2)], owned, v_send.at[3], v_recv.at[3])
        pending.append((yo.at[:, pl.ds(0, (nz - 1) * zb), :], v_send.at[3]))

    def owned_end():
        wait(yo.at[:, pl.ds(0, (nr - 1) * pb), :], v_recv.at[1])
        wait(ya.at[0, :, 0], in_sem.at[3])
        wait(yo.at[:, pl.ds(0, (nz - 1) * zb), :], v_recv.at[3])
        wait(yd.at[pl.ds(0, 2)], in_sem.at[5])

    def chol_start(gram):
        ae[:, 0:LANES] = gram
        eye = iota((LANES, LANES), 0) == iota((LANES, LANES), 1)
        ae[:, LANES:] = eye.astype(jnp.float32)

    tiles = range(PIVOTS // 8)
    sub = [iota((8, LANES), 0) + 8 * g for g in tiles]
    lane = iota((PIVOTS, LANES), 1)

    def over_rows(x, t):
        return jnp.broadcast_to(x[t:t + 1, :], (8, LANES))

    def chol_blocks(lo, hi):
        @pl.loop(lo, hi)
        def _(b):
            at = pl.multiple_of(b * PIVOTS, PIVOTS)
            turned = pltpu.roll(ae[pl.ds(at, PIVOTS), 0:LANES], (LANES - b * PIVOTS) % LANES, 1)
            d = [turned[8 * g:8 * g + 8] for g in tiles]
            e = [ae[pl.ds(at + 8 * g, 8), LANES:] for g in tiles]
            cols = [[jnp.broadcast_to(d[g][:, t:t + 1], (8, LANES)) for g in tiles] for t in range(PIVOTS)]
            scale = [jnp.zeros((8, LANES), jnp.float32) for g in tiles]
            for t in range(PIVOTS):
                g0, t0 = t // 8, t % 8
                pivot = over_rows(cols[t][g0], t0)
                r = pltpu.reciprocal(pivot, approx=True)
                r = r * (2.0 - pivot * r)
                f = {g: cols[t][g] * r for g in tiles if g >= g0}
                f[g0] = jnp.where(sub[g0] > t, f[g0], 0.0)
                scale[g0] = jnp.where(sub[g0] == t, lax.rsqrt(pivot), scale[g0])
                for u in range(t + 1, PIVOTS):
                    row = over_rows(cols[u][g0], t0)
                    for g in f:
                        cols[u][g] = cols[u][g] - f[g] * row
                d_row, e_row = over_rows(d[g0], t0), over_rows(e[g0], t0)
                for g in f:
                    d[g] = d[g] - f[g] * d_row
                    e[g] = e[g] - f[g] * e_row
            rows = pltpu.roll(jnp.concatenate([d[g] * scale[g] for g in tiles], axis=0), b * PIVOTS, 1)
            inverse = jnp.concatenate([e[g] * scale[g] for g in tiles], axis=0)
            later = jnp.where(lane >= b * PIVOTS + PIVOTS, rows, 0.0)
            ae[...] -= mm_tn_stacked(later, jnp.concatenate([rows, inverse], axis=1))
            ae[pl.ds(at, PIVOTS), LANES:] = inverse

    def exchange_begin(n):
        to_core(sx.at[n], sr.at[n], x_send.at[n], x_recv.at[n])
        pending.append((sr.at[n], x_send.at[n]))

    def reduce_1(n, product):
        for dy in sorted(range(gy), key=lambda d: -min(d, gy - d)):
            block = pl.ds(pl.multiple_of(ys[dy] * bi, 8), gx * bi)
            part[n, block, :] = product(jnp.concatenate([yb[0, block, :], yb[1, block, :]], axis=1))
            peers = [ys[dy] + xs[dx] for dx in sorted(range(gx), key=lambda d: -min(d, gx - d)) if dx or dy]
            to_xy(lambda p: part.at[n, pl.ds(pl.multiple_of(p * bi, 8), bi), :], r1.at[n, m], r1_send.at[n], r1_recv.at[n], peers)
        pending.append((r1.at[n, pl.ds(0, nr - 1)], r1_send.at[n]))
        r1[n, m] = part[n, pl.ds(pl.multiple_of(m * bi, 8), bi), :]

    def reduce_2(n):
        wait(r1.at[n, pl.ds(0, nr - 1)], r1_recv.at[n])
        total = r1[n, 0]
        for k in range(1, nr):
            total = total + r1[n, k]
        s1[n] = total
        to_z(lambda p: s1.at[n], r2.at[n, z], r2_send.at[n], r2_recv.at[n])
        pending.append((r2.at[n, pl.ds(0, nz - 1)], r2_send.at[n]))
        r2[n, z] = total

    def reduce_3(n):
        wait(r2.at[n, pl.ds(0, nz - 1)], r2_recv.at[n])
        total = r2[n, 0]
        for k in range(1, nz):
            total = total + r2[n, k]
        s2[n] = total
        mine = pl.ds(pl.multiple_of(m * bi, 8), bi)
        to_xy(lambda p: s2.at[n], im.at[n, mine, :], r3_send.at[n], r3_recv.at[n])
        pending.append((im.at[n, pl.ds(0, (nr - 1) * bi), :], r3_send.at[n]))
        im[n, mine, :] = total

    def reduce_end(n):
        wait(im.at[n, pl.ds(0, (nr - 1) * bi), :], r3_recv.at[n])

    def unfolded():
        return jnp.concatenate([yb[0], yb[1]], axis=1)

    both = mm3(f0t[...], unfolded())
    for p in range(2):
        sx[0, p] = both[:, p * LANES:(p + 1) * LANES]
    exchange_begin(0)
    wait(sr.at[0], x_recv.at[0])
    small = jnp.concatenate([sx[0, p] + sr[0, p] for p in range(2)], axis=1)
    reduce_1(0, lambda rows: mm3(rows, small, ((1,), (1,))))
    owned_z(0)
    yt[0] = yb[0].T
    reduce_2(0)
    ring_owned_xy()
    yt[1] = yb[1].T
    reduce_3(0)
    owned_z(1)
    reduce_end(0)

    sx[1] = mm3(yt[...].reshape(2 * LANES, il), im[0]).reshape(2, LANES, LANES)
    exchange_begin(1)
    gx_s[0] = mm_tn(im[0], im[0])
    to_core(gx_s.at[0], gr.at[0], g_send.at[0], g_recv.at[0])
    pending.append((gr.at[0], g_send.at[0]))
    wait(sr.at[1], x_recv.at[1])
    small = (sx[1] + sr[1]).reshape(2 * LANES, LANES)
    reduce_1(1, lambda rows: mm3(rows, small))
    owned_z(2)
    blocks = LANES // PIVOTS
    wait(gr.at[0], g_recv.at[0])
    chol_start(gx_s[0] + gr[0])
    chol_blocks(0, 1)
    reduce_2(1)
    owned_xy()
    chol_blocks(1, 3)
    reduce_3(1)
    ring_owned_z()
    chol_blocks(3, blocks)
    linv[...] = ae[:, LANES:]
    reduce_end(1)
    images = mm_nt(im[1], linv[...])
    gx_s[1] = mm_tn(images, images)
    to_core(gx_s.at[1], gr.at[1], g_send.at[1], g_recv.at[1])
    pending.append((gr.at[1], g_send.at[1]))

    owned_end()
    sx[2] = mm_tn(jnp.concatenate([yo[0], yo[1]], axis=1), images).reshape(2, LANES, LANES)
    exchange_begin(2)
    wait(gr.at[1], g_recv.at[1])
    chol_start(gx_s[1] + gr[1])
    chol_blocks(0, blocks)
    wait(sr.at[2], x_recv.at[2])
    core = mm_nt(ae[:, LANES:], (sx[2] + sr[2]).reshape(2 * LANES, LANES))
    for q in range(2):
        out_ref[:, q, :] = core[:, q * LANES:(q + 1) * LANES]
    finish()


def solution(mesh):
    nr, nz = mesh.shape["rad"], mesh.shape["span"]
    gx = 1
    while gx * gx < nr:
        gx *= 2

    def body(tensor, radial_factor, span_factor, start_factor):
        il = start_factor.shape[0]
        pb = il // nr - il // nr // 4
        zb = (il - nr * pb) // nz
        nc, ng, nq, nh = pb // CHUNK, pb // GROUP, zb // CHUNK, zb // GROUP
        bi = il // nr
        f32 = jnp.float32
        dma = pltpu.SemaphoreType.DMA
        vm = lambda *s: pltpu.VMEM(s, f32)
        scratch = [
            vm(*radial_factor.shape), vm(*span_factor.shape), vm(*start_factor.shape),
            vm(nc, nr, CHUNK * 16, LANES),
            vm(nr, 8, LANES), vm(nz, 8, LANES),
            vm(nz * 8, nr * 16), vm(nr * 16, nz * 64),
            vm(ng, nz, GROUP * 8, LANES), vm(ng, nz, GROUP * 8, LANES),
            vm(ng, nr, 2, GROUP, LANES),
            vm(2, il, LANES), vm(2, LANES, il), vm(LANES, il),
            vm(3, 2, LANES, LANES), vm(3, 2, LANES, LANES),
            vm(2, il, LANES),
            vm(2, nr, bi, LANES), vm(2, bi, LANES),
            vm(2, nz, bi, LANES), vm(2, bi, LANES),
            vm(2, il, LANES),
            vm(2, LANES, LANES), vm(2, LANES, LANES),
            vm(LANES, 2 * LANES), vm(LANES, LANES),
            vm(nz, 2, 2, pb, LANES), vm(2, il, LANES), vm(nr, zb, LANES),
            vm(nq, nz, CHUNK * 16, LANES), vm(nr * 8, nz * 32), vm(nz * 16, nr * 32),
            vm(nr, zb * 4, LANES), vm(nr, zb * 4, LANES), vm(nz * 2, zb, LANES),
            dma((6,)), dma((7, nc)),
            dma((2,)), dma((2,)),
            dma, dma((nc,)),
            dma, dma((nc,)),
            dma, dma,
            dma((3,)), dma((3,)),
            dma((2,)), dma((2,)),
            dma((2,)), dma((2,)), dma((2,)), dma((2,)), dma((2,)), dma((2,)),
            dma((4,)), dma((4,)),
            dma((3,)), dma((nq + 1,)), dma((nh,)),
        ]
        rows = tensor.reshape(il * 16, LANES)
        hbm = pl.BlockSpec(memory_space=pltpu.HBM)
        core = pl.pallas_call(
            functools.partial(kernel, nr, nz, gx),
            out_shape=jax.ShapeDtypeStruct((LANES, 2, LANES), f32),
            in_specs=[hbm] * 4,
            out_specs=pl.BlockSpec(memory_space=pltpu.VMEM),
            scratch_shapes=scratch,
            compiler_params=pltpu.CompilerParams(collective_id=0, has_side_effects=True, vmem_limit_bytes=62 * 1024 * 1024),
        )(rows, radial_factor, span_factor, start_factor)
        return core.reshape(LANES, 1, 2, LANES)

    in_specs = (P("ax", "rad", "span", None), P("rad", None), P("span", None), P("ax", None))
    out_specs = P(None, "rad", "span", None)
    return jax.shard_map(body, mesh=mesh, in_specs=in_specs, out_specs=out_specs, check_vma=False)
```
